256 devices in a mesh: blk: 16 (over z, y_hi), tp: 4 (over y_lo, core), enc: 4 (over x).
Axes of the slice: x: 4, y: 4 (y_hi: 2, y_lo: 2; y = y_hi * 2 + y_lo), z: 8, core: 2. Of those that a mesh axis runs over, the one named last changes fastest.
Arguments:
- self_query_columns: bfloat16 [8192, 4096], P('blk', ('tp', 'enc')), may hold values from -12 to 12
- text_key_value: bfloat16 [8192, 2, 512], P('blk', None, 'tp'), may hold values from -9 to 9
- cross_query_columns: bfloat16 [8192, 4096], P('blk', ('tp', 'enc')), may hold values from -12 to 12
- image_kv: bfloat16 [16, 2, 6404, 512], P('blk', None, 'enc', 'tp'), may hold values from -9 to 9
- block_images: int32 [64, 16], P('blk'), may hold values from 0 to 1, as said below
- image_owner: int32 [16], replicated, may hold values from 0 to 15, each once
Outputs:
- self_out: bfloat16 [8192, 4096], P('blk', ('tp', 'enc'))
- cross_out: bfloat16 [8192, 4096], P('blk', ('tp', 'enc'))
The draws below stay inside these ranges and needn't reach their ends.
Inputs may be any that keep to these rules, and one draw needn't show every extreme that they name: `block_images`: each block of 128 text tokens sees one or two images: the image most recently placed before it and, in some blocks, the image placed before that one. Image ids rise along the text, every image is seen by some block, and some block sees two. A permutation: image i's keys and values are slot image_owner[i] of image_kv.
All inputs are finite; a program needn't handle non-finite values.
Results may differ from the reference program's by a relative error of at most 0.007.
Values may be sent and summed in bfloat16 or wider, within the bound.
A program may use at most 64 MiB of HBM per device.

```python
import math
import jax
import jax.numpy as jnp
from jax import lax

QUERY_HEADS = 32
KEY_VALUE_HEADS = 4
HEAD_SIZE = 128
IMAGE_TOKENS = 6404
MASK_BLOCK_TOKENS = 128
TEXT_TOKENS = 8192
MASK_BLOCK_COUNT = 64
IMAGE_COUNT = 16


def draw_self_query_columns(key, part):
    key = jax.random.fold_in(key, 11)
    drawn_result = 2.5 * jnp.clip(jax.random.normal(key, (TEXT_TOKENS, QUERY_HEADS, HEAD_SIZE), jnp.float32), -4.0, 4.0)
    return drawn_result.reshape(TEXT_TOKENS, QUERY_HEADS * HEAD_SIZE).astype(jnp.bfloat16)


def draw_cross_query_columns(key, part):
    key = jax.random.fold_in(key, 23)
    drawn_result = 2.5 * jnp.clip(jax.random.normal(key, (TEXT_TOKENS, QUERY_HEADS, HEAD_SIZE), jnp.float32), -4.0, 4.0)
    return drawn_result.reshape(TEXT_TOKENS, QUERY_HEADS * HEAD_SIZE).astype(jnp.bfloat16)


def draw_text_key_value(key, part):
    key = jax.random.fold_in(key, 37)
    drawn_result = jnp.clip(jax.random.normal(key, (TEXT_TOKENS, 2, KEY_VALUE_HEADS, HEAD_SIZE), jnp.float32), -4.0, 4.0)
    return drawn_result.reshape(TEXT_TOKENS, 2, KEY_VALUE_HEADS * HEAD_SIZE).astype(jnp.bfloat16)


def draw_image_kv(key, part):
    key = jax.random.fold_in(key, 44)
    drawn_result = jnp.clip(jax.random.normal(key, (IMAGE_COUNT, 2, IMAGE_TOKENS, KEY_VALUE_HEADS, HEAD_SIZE), jnp.float32), -4.0, 4.0)
    return drawn_result.reshape(IMAGE_COUNT, 2, IMAGE_TOKENS, KEY_VALUE_HEADS * HEAD_SIZE).astype(jnp.bfloat16)


def draw_block_images(key, part):
    key = jax.random.fold_in(key, 59)
    order = jax.random.permutation(jax.random.fold_in(key, 1), MASK_BLOCK_COUNT - 1) + 1
    cuts = order[:IMAGE_COUNT - 1]
    is_cut = jnp.zeros((MASK_BLOCK_COUNT,), jnp.int32).at[cuts].set(1)
    current = jnp.cumsum(is_cut).astype(jnp.int32)
    second = jax.random.randint(jax.random.fold_in(key, 2), (MASK_BLOCK_COUNT,), 0, 4) > 0
    second = second & (current > 0)
    second = second.at[MASK_BLOCK_COUNT - 1].set(True)
    image_ids = jnp.arange(IMAGE_COUNT, dtype=jnp.int32)
    latest = image_ids[None, :] == current[:, None]
    before = second[:, None] & (image_ids[None, :] == current[:, None] - 1)
    return (latest | before).astype(jnp.int32)


def setup_inputs(seed: int = 0) -> dict:
    seeds = jax.random.split(jax.random.key(seed), 7)
    return {
        "self_query_columns": draw_self_query_columns(jax.random.fold_in(seeds[6], 71), 0),
        "text_key_value": draw_text_key_value(jax.random.fold_in(seeds[6], 71), 0),
        "cross_query_columns": draw_cross_query_columns(jax.random.fold_in(seeds[6], 71), 0),
        "image_kv": draw_image_kv(jax.random.fold_in(seeds[6], 71), 0),
        "block_images": draw_block_images(jax.random.fold_in(seeds[6], 71), 0),
        "image_owner": jax.random.permutation(seeds[5], IMAGE_COUNT).astype(jnp.int32),
    }


def attend_rows(queries, key_row_block, value_row_block, allowed):
    scores = jnp.einsum('rkgd,tkd->kgrt', queries, key_row_block) * (1.0 / math.sqrt(HEAD_SIZE))
    scores = jnp.where(allowed, scores, -1e+30)
    highest = lax.optimization_barrier(jnp.max(scores, axis=-1, keepdims=True))
    weights = jnp.where(allowed, jnp.exp(scores - highest), 0.0)
    totals = lax.optimization_barrier(jnp.sum(weights, axis=-1))
    rounded = lax.optimization_barrier(weights.astype(jnp.bfloat16)).astype(jnp.float32)
    mixed = jnp.einsum('kgrt,tkd->rkgd', rounded, value_row_block)
    mixed = mixed / jnp.transpose(totals, (2, 0, 1))[..., None]
    return mixed.reshape(queries.shape[0], QUERY_HEADS * HEAD_SIZE).astype(jnp.bfloat16)

def reference(self_query_columns, text_key_value, cross_query_columns, image_kv, block_images, image_owner):
    query_group_width = QUERY_HEADS // KEY_VALUE_HEADS
    key_row_block = text_key_value[:, 0].astype(jnp.float32).reshape(TEXT_TOKENS, KEY_VALUE_HEADS, HEAD_SIZE)
    value_row_block = text_key_value[:, 1].astype(jnp.float32).reshape(TEXT_TOKENS, KEY_VALUE_HEADS, HEAD_SIZE)
    key_pos = jnp.arange(TEXT_TOKENS, dtype=jnp.int32)
    self_block_list = self_query_columns.reshape(MASK_BLOCK_COUNT, MASK_BLOCK_TOKENS, KEY_VALUE_HEADS, query_group_width, HEAD_SIZE)

    def self_block(element):
        queries, block_index = element
        query_pos = block_index * MASK_BLOCK_TOKENS + jnp.arange(MASK_BLOCK_TOKENS, dtype=jnp.int32)
        allowed = key_pos[None, :] <= query_pos[:, None]
        return attend_rows(queries.astype(jnp.float32), key_row_block, value_row_block, allowed)
    self_out = lax.map(self_block, (self_block_list, jnp.arange(MASK_BLOCK_COUNT, dtype=jnp.int32)))
    self_out = self_out.reshape(TEXT_TOKENS, QUERY_HEADS * HEAD_SIZE)
    image_ids = jnp.arange(IMAGE_COUNT, dtype=jnp.int32)
    cross_block_list = cross_query_columns.reshape(MASK_BLOCK_COUNT, MASK_BLOCK_TOKENS, KEY_VALUE_HEADS, query_group_width, HEAD_SIZE)

    def cross_block(element):
        queries, seen = element
        latest = jnp.max(jnp.where(seen > 0, image_ids, -1)).astype(jnp.int32)
        earlier = jnp.max(jnp.where((seen > 0) & (image_ids < latest), image_ids, -1)).astype(jnp.int32)
        first_slot = image_owner[latest].astype(jnp.int32)
        second_slot = image_owner[jnp.maximum(earlier, 0)].astype(jnp.int32)
        first_image = lax.dynamic_index_in_dim(image_kv, first_slot, 0, keepdims=False)
        second_image = lax.dynamic_index_in_dim(image_kv, second_slot, 0, keepdims=False)
        joined_parts = jnp.concatenate([first_image, second_image], axis=1).astype(jnp.float32)
        key_section = joined_parts[0].reshape(2 * IMAGE_TOKENS, KEY_VALUE_HEADS, HEAD_SIZE)
        value_section = joined_parts[1].reshape(2 * IMAGE_TOKENS, KEY_VALUE_HEADS, HEAD_SIZE)
        allowed = jnp.concatenate([jnp.ones((IMAGE_TOKENS,), dtype=jnp.bool_), jnp.full((IMAGE_TOKENS,), earlier >= 0)])
        return attend_rows(queries.astype(jnp.float32), key_section, value_section, allowed)
    cross_out = lax.map(cross_block, (cross_block_list, block_images))
    cross_out = cross_out.reshape(TEXT_TOKENS, QUERY_HEADS * HEAD_SIZE)
    return (self_out, cross_out)
```

```python
import functools
import math

import jax
import jax.numpy as jnp
from jax import lax
from jax.experimental import pallas as pl
from jax.experimental.pallas import tpu as pltpu
from jax.sharding import PartitionSpec as P

MESH = pl.DeviceIdType.MESH
BF = jnp.bfloat16
F32 = jnp.float32
LAYERS = 8
ENC = 4
HEAD = 128
BLOCK = 128
ROWS = 512
TOKENS = 1601
HALF = 816
FIRST = 512
SECOND = 304
LAST_VALID = TOKENS - HALF - FIRST
NEG = -1e30
EXP_SCALE = math.log2(math.e) / math.sqrt(HEAD)
TILE = 512


def dot_t(a, b):
    return lax.dot_general(a, b, (((1,), (1,)), ((), ())), preferred_element_type=F32)


def weigh(p, v):
    ones = jnp.ones(v.shape, BF)
    return jnp.dot(p.astype(BF), jnp.concatenate([v, ones], axis=1), preferred_element_type=F32)


def kernel(
    sq_ref, text_ref, cq_ref, img_ref, seen_ref, owner_ref,
    self_out, cross_out,
    img_a, img_b, stage_a, stage_b, text, sq, cq, seen, seen_sm, pick, bias,
    acc, tot, top,
    s_part, s_lse, s_got, s_got_lse,
    c_part, c_lse, c_got, c_got_lse,
    za_s, za_r, zb_s, zb_r, tz_s, tz_r, ty_s, ty_r, y_s, y_r,
    sq_s, sq_r, cq_s, cq_r, so_s, so_r, sl_s, sl_r, co_s, co_r, cl_s, cl_r, local_sem,
):
    blk = lax.axis_index("blk")
    x = lax.axis_index("enc")
    z = blk // 2
    y = blk % 2
    partner = 2 * z + 1 - y

    def at(z_, y_, x_):
        return {"blk": 2 * z_ + y_, "enc": x_}

    def remote(src, dst, s, r, device):
        return pltpu.make_async_remote_copy(
            src_ref=src, dst_ref=dst, send_sem=s, recv_sem=r, device_id=device, device_id_type=MESH
        )

    sign = (1, -1)

    def layer(direction, distance):
        return (z - sign[direction] * distance + LAYERS) % LAYERS

    def onward(direction):
        return at((z + sign[direction] + LAYERS) % LAYERS, y, x)

    def unit(buf, s, r, direction, distance, order, sem):
        slot = 2 * layer(direction, distance) + (y + order) % 2
        return remote(
            buf.at[slot], buf.at[slot],
            s.at[direction, sem, order], r.at[direction, sem, order], onward(direction),
        )

    ring_a = (img_a, za_s, za_r)
    ring_b = (img_b, zb_s, zb_r)

    def send_own(ring, order):
        for direction in range(2):
            unit(*ring, direction, 0, order, 0).start()

    def ring_event(ring, distance, order):
        for direction in range(2):
            if distance == 4 and order != direction:
                continue
            unit(*ring, direction, distance, order, distance - 1).wait_recv()
            if distance < 3 or (distance == 3 and order == direction):
                unit(*ring, direction, distance, order, distance).start()

    def ring_last(ring):
        ring_event(ring, 4, 0)
        ring_event(ring, 4, 1)

    def ring_sent(ring):
        for direction in range(2):
            for distance in range(4):
                for order in range(2):
                    if distance < 3 or order == direction:
                        unit(*ring, direction, distance, order, distance).wait_send()

    def text_unit(direction, distance, sem):
        chunk = 2 * layer(direction, distance) + y
        return remote(
            text.at[chunk], text.at[chunk],
            tz_s.at[direction, sem], tz_r.at[direction, sem], onward(direction),
        )

    def text_across(chunk_layer, y_):
        chunk = 2 * chunk_layer + y_
        return remote(
            text.at[chunk], text.at[chunk], ty_s.at[chunk_layer], ty_r.at[chunk_layer],
            {"blk": partner},
        )

    def text_event(distance):
        for direction in range(2):
            if distance == 4 and direction == 1:
                continue
            text_unit(direction, distance, distance - 1).wait_recv()
            if distance < 3 or (distance == 3 and direction == 0):
                text_unit(direction, distance, distance).start()
            text_across(layer(direction, distance), y).start()

    def peer(step):
        return (x + step) % ENC

    def sq_copy(step):
        return remote(sq.at[x], sq.at[x], sq_s.at[step], sq_r.at[x], at(z, y, peer(step)))

    def cq_copy(flip, step):
        return remote(
            cq.at[x, y], cq.at[x, y], cq_s.at[flip, step], cq_r.at[x, y],
            at(z, (y + flip) % 2, peer(step)),
        )

    def half_copy(stage, buf, which):
        slot = 2 * z + y
        return remote(stage, buf.at[slot], y_s.at[which], y_r.at[which], {"blk": partner})

    def half_wait(stage, buf, which):
        slot = 2 * z + 1 - y
        remote(stage, buf.at[slot], y_s.at[which], y_r.at[which], {"blk": partner}).wait_recv()

    seen_copy = remote(seen.at[y], seen.at[y], y_s.at[2], y_r.at[2], {"blk": partner})

    def take_half(first, second, half):
        base = half * HALF
        for kv in range(2):
            first[kv] = img_ref[kv, base : base + FIRST, :]
            start = base + FIRST
            if half == 0:
                second[kv] = img_ref[kv, start : start + SECOND, :]
            else:
                whole = (LAST_VALID // 16) * 16
                second[kv, 0:whole, :] = img_ref[kv, start : start + whole, :]
                row = img_ref[kv, TOKENS - 1 : TOKENS, :].astype(F32)
                at_row = lax.broadcasted_iota(jnp.int32, (16, HEAD), 0)
                tail = jnp.where(at_row == 0, jnp.broadcast_to(row, (16, HEAD)), 0.0)
                second[kv, whole : whole + 16, :] = tail.astype(BF)
                second[kv, whole + 16 : SECOND, :] = jnp.zeros((SECOND - whole - 16, HEAD), BF)

    own = 2 * z + y
    for column in range(2):

        @pl.when(y == column)
        def _():
            take_half(img_a.at[own], img_b.at[own], column)
            take_half(stage_a, stage_b, 1 - column)

    text[own] = text_ref[...]
    sq[x] = sq_ref[...]
    cq[x, y] = cq_ref[...]
    seen[y] = jnp.zeros((8, 128), jnp.int32)
    seen[y, 0:4, 0:16] = seen_ref[...]

    barrier = pltpu.get_barrier_semaphore()
    for flip in range(2):
        for step in range(ENC):
            if flip or step:
                pl.semaphore_signal(
                    barrier, inc=1, device_id=at(z, (y + flip) % 2, peer(step)), device_id_type=MESH
                )
    for direction in range(2):
        pl.semaphore_signal(barrier, inc=1, device_id=onward(direction), device_id_type=MESH)
    pl.semaphore_wait(barrier, 9)

    for direction in range(2):
        text_unit(direction, 0, 0).start()
    half_copy(stage_a, img_a, 0).start()
    text_across(z, y).start()
    send_own(ring_a, 0)
    for step in (1, 3, 2):
        sq_copy(step).start()
    seen_copy.start()
    half_copy(stage_b, img_b, 1).start()
    for flip, step in ((0, 1), (0, 3), (1, 0), (0, 2), (1, 1), (1, 3), (1, 2)):
        cq_copy(flip, step).start()

    text_event(1)
    half_wait(stage_a, img_a, 0)
    send_own(ring_a, 1)
    text_event(2)
    ring_event(ring_a, 1, 0)
    text_event(3)
    text_event(4)
    ring_event(ring_a, 1, 1)
    ring_event(ring_a, 2, 0)
    for k in range(LAYERS):
        text_across(k, 1 - y).wait_recv()
    for step in (1, 2, 3):
        other = peer(step)
        remote(sq.at[other], sq.at[other], sq_s.at[step], sq_r.at[other], at(z, y, other)).wait_recv()

    diagonal = lax.broadcasted_iota(jnp.int32, (BLOCK, BLOCK), 0) == lax.broadcasted_iota(
        jnp.int32, (BLOCK, BLOCK), 1
    )

    def rows_of(ref, first_x, rows):
        return jnp.concatenate(
            [ref[first_x + k // 2, rows, (k % 2) * HEAD : (k % 2 + 1) * HEAD] for k in range(4)], axis=0
        )

    def put(part, lse, block, half, o, level):
        for k in range(4):
            t = 2 * half + k // 2
            lanes = slice((k % 2) * HEAD, (k % 2 + 1) * HEAD)
            part[block, t, :, lanes] = o[k * BLOCK : (k + 1) * BLOCK].astype(BF)
            square = jnp.where(diagonal, level[k * BLOCK : (k + 1) * BLOCK], 0.0)
            lse[block, t, k % 2 : k % 2 + 1, :] = jnp.sum(square, axis=0, keepdims=True)

    def s_copies(rb, step):
        t = peer(step)
        device = at(z, y, t)
        return (
            remote(s_part.at[rb, t], s_got.at[x, rb], so_s.at[rb, step], so_r.at[x, rb], device),
            remote(s_lse.at[rb, t], s_got_lse.at[x, rb], sl_s.at[rb, step], sl_r.at[x, rb], device),
        )

    def self_step(i):
        rb = i // 2
        half = i % 2
        rows = pl.ds(pl.multiple_of(rb * BLOCK, BLOCK), BLOCK)
        q = rows_of(sq, 2 * half, rows)
        keys = text[:, :, 0:HEAD].reshape(16 * BLOCK, HEAD)
        values = text[:, :, HEAD:].reshape(16 * BLOCK, HEAD)
        s = dot_t(q, keys)
        row = lax.broadcasted_iota(jnp.int32, (TILE, 1), 0) % BLOCK
        inside = jnp.where(x < rb, BLOCK, jnp.where(x == rb, row + 1, 0))
        limit = blk * BLOCK + inside
        index = lax.broadcasted_iota(jnp.int32, s.shape, 1)
        s = jnp.where(index < limit, s, NEG)
        m = jnp.max(s, axis=1, keepdims=True) * EXP_SCALE
        pv = weigh(jnp.exp2(s * EXP_SCALE - m), values)
        total = pv[:, HEAD:]
        put(s_part, s_lse, rb, half, pv[:, :HEAD] / total, m + jnp.log2(total))

        @pl.when(half == 1)
        def _():
            s_got[x, rb] = s_part[rb, x]
            s_got_lse[x, rb] = s_lse[rb, x]
            for step in (1, 3, 2):
                for copy in s_copies(rb, step):
                    copy.start()

    def self_loop(i, carry):
        @pl.when(i == 0)
        def _():
            ring_event(ring_a, 2, 1)

        @pl.when(i == 2)
        def _():
            ring_event(ring_a, 3, 0)
            send_own(ring_b, 0)

        @pl.when(i == 5)
        def _():
            ring_event(ring_a, 3, 1)
            half_wait(stage_b, img_b, 1)
            send_own(ring_b, 1)

        self_step(i)
        return carry

    lax.fori_loop(0, 8, self_loop, 0)
    ring_last(ring_a)

    remote(seen.at[1 - y], seen.at[1 - y], y_s.at[2], y_r.at[2], {"blk": partner}).wait_recv()
    to_scalar = pltpu.make_async_copy(seen, seen_sm, local_sem)
    to_scalar.start()
    to_scalar.wait()

    def choose(b, carry):
        latest = jnp.int32(0)
        earlier = jnp.int32(0)
        count = jnp.int32(0)
        for i in range(16):
            flag = seen_sm[b // 4, b % 4, i] > 0
            slot = owner_ref[i]
            earlier = jnp.where(jnp.logical_and(flag, count == 0), slot, earlier)
            latest = jnp.where(flag, slot, latest)
            count = count + jnp.where(flag, 1, 0)
        pick[b, 0] = latest
        pick[b, 1] = earlier
        bias[b] = jnp.where(count > 1, 0.0, NEG)
        return carry

    lax.fori_loop(0, 8, choose, 0)
    for flip in range(2):
        for step in range(ENC):
            if flip or step:
                ox, oy = peer(step), (y + flip) % 2
                remote(
                    cq.at[ox, oy], cq.at[ox, oy], cq_s.at[flip, step], cq_r.at[ox, oy], at(z, oy, ox)
                ).wait_recv()

    def cross_query(i):
        chunk = (i // 2) % 2
        rb = i // 4
        half = i % 2
        rows = pl.ds(pl.multiple_of(rb * BLOCK, BLOCK), BLOCK)
        q = jnp.concatenate(
            [
                cq[2 * half + k // 2, chunk, rows, (k % 2) * HEAD : (k % 2 + 1) * HEAD]
                for k in range(4)
            ],
            axis=0,
        )
        return chunk, rb, half, q

    def first_step(i):
        chunk, rb, half, q = cross_query(i)
        b = chunk * 4 + rb
        one, two, off = pick[b, 0], pick[b, 1], bias[b]
        s1 = dot_t(q, img_a[one, 0])
        s2 = dot_t(q, img_a[two, 0])
        m = jnp.maximum(
            jnp.max(s1, axis=1, keepdims=True) * EXP_SCALE,
            jnp.max(s2, axis=1, keepdims=True) * EXP_SCALE + off,
        )
        pv = weigh(jnp.exp2(s1 * EXP_SCALE - m), img_a[one, 1])
        pv = pv + weigh(jnp.exp2(s2 * EXP_SCALE - (m - off)), img_a[two, 1])
        acc[i] = pv[:, :HEAD]
        tot[i] = pv[:, HEAD:]
        top[i] = m

    def first_loop(i, carry):
        for k in range(5):

            @pl.when(i == 2 + 3 * k)
            def _():
                ring_event(ring_b, 1 + k // 2, k % 2)

        first_step(i)
        return carry

    lax.fori_loop(0, 16, first_loop, 0)

    def combine(got, got_lse, sources, block, out, rows):
        for hh in range(2):
            lanes = slice(hh * HEAD, (hh + 1) * HEAD)
            levels = []
            for k in range(sources):
                line = jnp.broadcast_to(got_lse[k, block, hh : hh + 1, :], (BLOCK, BLOCK))
                levels.append(jnp.sum(jnp.where(diagonal, line, 0.0), axis=1, keepdims=True))
            high = functools.reduce(jnp.maximum, levels)
            shares = [jnp.exp2(level - high) for level in levels]
            total = functools.reduce(jnp.add, shares)
            mixed = functools.reduce(
                jnp.add,
                [
                    got[k, block, :, lanes].astype(F32) * (share / total)
                    for k, share in enumerate(shares)
                ],
            )
            out[rows, lanes] = mixed.astype(BF)

    def self_combine(rb, carry):
        for step in (1, 2, 3):
            o = peer(step)
            device = at(z, y, o)
            remote(s_part.at[rb, o], s_got.at[o, rb], so_s.at[rb, step], so_r.at[o, rb], device).wait_recv()
            remote(s_lse.at[rb, o], s_got_lse.at[o, rb], sl_s.at[rb, step], sl_r.at[o, rb], device).wait_recv()
        combine(s_got, s_got_lse, 4, rb, self_out, pl.ds(pl.multiple_of(rb * BLOCK, BLOCK), BLOCK))
        return carry

    lax.fori_loop(0, 4, self_combine, 0)
    ring_event(ring_b, 3, 1)
    ring_last(ring_b)

    def c_copies(b, chunk, rb, step):
        t = peer(step)
        device = at(z, chunk, t)
        source = 2 * x + y
        return (
            remote(c_part.at[b, t], c_got.at[source, rb], co_s.at[b, step], co_r.at[source, rb], device),
            remote(c_lse.at[b, t], c_got_lse.at[source, rb], cl_s.at[b, step], cl_r.at[source, rb], device),
        )

    valid = jnp.where(y == 0, SECOND, LAST_VALID)

    def second_loop(i, carry):
        chunk, rb, half, q = cross_query(i)
        b = chunk * 4 + rb
        one, two, off = pick[b, 0], pick[b, 1], bias[b]
        keep = lax.broadcasted_iota(jnp.int32, (TILE, SECOND), 1) < valid
        s1 = jnp.where(keep, dot_t(q, img_b[one, 0]), NEG)
        s2 = jnp.where(keep, dot_t(q, img_b[two, 0]), NEG)
        before = top[i]
        m = jnp.maximum(
            jnp.max(s1, axis=1, keepdims=True) * EXP_SCALE,
            jnp.max(s2, axis=1, keepdims=True) * EXP_SCALE + off,
        )
        m = jnp.maximum(m, before)
        fade = jnp.exp2(before - m)
        pv = weigh(jnp.exp2(s1 * EXP_SCALE - m), img_b[one, 1])
        pv = pv + weigh(jnp.exp2(s2 * EXP_SCALE - (m - off)), img_b[two, 1])
        total = tot[i] * fade + pv[:, HEAD:]
        put(c_part, c_lse, b, half, (acc[i] * fade + pv[:, :HEAD]) / total, m + jnp.log2(total))

        @pl.when(half == 1)
        def _():
            for step in (2, 1, 3):
                for copy in c_copies(b, chunk, rb, step):
                    copy.start()

            @pl.when(chunk == y)
            def _():
                c_got[2 * x + y, rb] = c_part[b, x]
                c_got_lse[2 * x + y, rb] = c_lse[b, x]

            @pl.when(chunk != y)
            def _():
                for copy in c_copies(b, chunk, rb, 0):
                    copy.start()

        return carry

    lax.fori_loop(0, 16, second_loop, 0)

    def cross_combine(rb, carry):
        for flip in range(2):
            for step in range(ENC):
                if flip or step:
                    ox, oy = peer(step), (y + flip) % 2
                    o = 2 * ox + oy
                    device = at(z, oy, ox)
                    remote(
                        c_part.at[rb, ox], c_got.at[o, rb], co_s.at[rb, step], co_r.at[o, rb], device
                    ).wait_recv()
                    remote(
                        c_lse.at[rb, ox], c_got_lse.at[o, rb], cl_s.at[rb, step], cl_r.at[o, rb], device
                    ).wait_recv()
        combine(c_got, c_got_lse, 8, rb, cross_out, pl.ds(pl.multiple_of(rb * BLOCK, BLOCK), BLOCK))
        return carry

    lax.fori_loop(0, 4, cross_combine, 0)

    ring_sent(ring_a)
    ring_sent(ring_b)
    for direction in range(2):
        for distance in range(4):
            if distance < 3 or direction == 0:
                text_unit(direction, distance, distance).wait_send()
    for k in range(LAYERS):
        text_across(k, y).wait_send()
    half_copy(stage_a, img_a, 0).wait_send()
    half_copy(stage_b, img_b, 1).wait_send()
    seen_copy.wait_send()
    for step in (1, 2, 3):
        sq_copy(step).wait_send()
    for flip in range(2):
        for step in range(ENC):
            if flip or step:
                cq_copy(flip, step).wait_send()

    def results_sent(rb, carry):
        for step in (1, 2, 3):
            for copy in s_copies(rb, step):
                copy.wait_send()
            for chunk in range(2):
                for copy in c_copies(chunk * 4 + rb, chunk, rb, step):
                    copy.wait_send()
        for copy in c_copies((1 - y) * 4 + rb, 1 - y, rb, 0):
            copy.wait_send()
        return carry

    lax.fori_loop(0, 4, results_sent, 0)


def per_device(self_query, text_kv, cross_query, image_kv, block_images, image_owner):
    quarter = lax.dynamic_slice_in_dim(text_kv, lax.axis_index("enc") * BLOCK, BLOCK, 0)
    quarter = quarter.reshape(BLOCK, 2 * HEAD)
    vmem = pl.BlockSpec(memory_space=pltpu.VMEM)
    smem = pl.BlockSpec(memory_space=pltpu.SMEM)
    dma = pltpu.SemaphoreType.DMA
    out = jax.ShapeDtypeStruct((ROWS, 2 * HEAD), BF)
    return pl.pallas_call(
        kernel,
        out_shape=(out, out),
        in_specs=[vmem, vmem, vmem, vmem, vmem, smem],
        out_specs=(vmem, vmem),
        scratch_shapes=[
            pltpu.VMEM((16, 2, FIRST, HEAD), BF),
            pltpu.VMEM((16, 2, SECOND, HEAD), BF),
            pltpu.VMEM((2, FIRST, HEAD), BF),
            pltpu.VMEM((2, SECOND, HEAD), BF),
            pltpu.VMEM((16, BLOCK, 2 * HEAD), BF),
            pltpu.VMEM((ENC, ROWS, 2 * HEAD), BF),
            pltpu.VMEM((ENC, 2, ROWS, 2 * HEAD), BF),
            pltpu.VMEM((2, 8, 128), jnp.int32),
            pltpu.SMEM((2, 8, 128), jnp.int32),
            pltpu.SMEM((8, 2), jnp.int32),
            pltpu.SMEM((8,), F32),
            pltpu.VMEM((16, TILE, HEAD), F32),
            pltpu.VMEM((16, TILE, HEAD), F32),
            pltpu.VMEM((16, TILE, 1), F32),
            pltpu.VMEM((4, ENC, BLOCK, 2 * HEAD), BF),
            pltpu.VMEM((4, ENC, 8, HEAD), F32),
            pltpu.VMEM((ENC, 4, BLOCK, 2 * HEAD), BF),
            pltpu.VMEM((ENC, 4, 8, HEAD), F32),
            pltpu.VMEM((8, ENC, BLOCK, 2 * HEAD), BF),
            pltpu.VMEM((8, ENC, 8, HEAD), F32),
            pltpu.VMEM((8, 4, BLOCK, 2 * HEAD), BF),
            pltpu.VMEM((8, 4, 8, HEAD), F32),
            dma((2, 4, 2)), dma((2, 4, 2)), dma((2, 4, 2)), dma((2, 4, 2)),
            dma((2, 4)), dma((2, 4)), dma((LAYERS,)), dma((LAYERS,)),
            dma((3,)), dma((3,)),
            dma((ENC,)), dma((ENC,)), dma((2, ENC)), dma((ENC, 2)),
            dma((4, ENC)), dma((ENC, 4)), dma((4, ENC)), dma((ENC, 4)),
            dma((8, ENC)), dma((8, 4)), dma((8, ENC)), dma((8, 4)),
            dma,
        ],
        compiler_params=pltpu.CompilerParams(
            collective_id=0, has_side_effects=True, vmem_limit_bytes=60 * 2**20
        ),
        cost_estimate=pl.CostEstimate(
            flops=512 * 22_000_000, bytes_accessed=8_000_000, transcendentals=22_000_000
        ),
    )(self_query, quarter, cross_query, image_kv[0], block_images, image_owner)


def solution(mesh):
    spread = P("blk", ("tp", "enc"))
    return jax.shard_map(
        per_device,
        mesh=mesh,
        in_specs=(spread, P("blk", None, "tp"), spread, P("blk", None, "enc", "tp"), P("blk", None), P()),
        out_specs=(spread, spread),
        check_vma=False,
    )
```

```python
import functools
import math

import jax
import jax.numpy as jnp
from jax import lax
from jax.experimental import pallas as pl
from jax.experimental.pallas import tpu as pltpu
from jax.sharding import PartitionSpec as P

MESH = pl.DeviceIdType.MESH
BF = jnp.bfloat16
F32 = jnp.float32
LAYERS = 8
ENC = 4
HEAD = 128
BLOCK = 128
ROWS = 512
TOKENS = 1601
HALF = 816
FIRST = 512
SECOND = 304
WHOLE = 256
LAST_VALID = TOKENS - HALF - FIRST
NEG = -1e30
EXP_SCALE = math.log2(math.e) / math.sqrt(HEAD)
TILE = 256


def dot_t(a, b):
    return lax.dot_general(a, b, (((1,), (1,)), ((), ())), preferred_element_type=F32)


def weigh(p, v):
    ones = jnp.ones(v.shape, BF)
    return jnp.dot(p.astype(BF), jnp.concatenate([v, ones], axis=1), preferred_element_type=F32)


def kernel(
    sq_ref, text_ref, cq_ref, img_ref, seen_ref, owner_ref,
    self_out, cross_out,
    img_a, img_b, text, sq, cq, seen, seen_sm, pick, bias,
    acc, tot, top,
    s_part, s_lse, s_got, s_got_lse,
    c_part, c_lse, c_got, c_got_lse,
    za_s, za_r, zb_s, zb_r, tz_s, tz_r, ty_s, ty_r, y_s, y_r,
    sq_s, sq_r, cq_s, cq_r, so_s, so_r, sl_s, sl_r, co_s, co_r, cl_s, cl_r, local_sem, load_sem, store_sem, self_rows, cross_rows,
):
    blk = lax.axis_index("blk")
    x = lax.axis_index("enc")
    z = blk // 2
    y = blk % 2
    partner = 2 * z + 1 - y

    def at(z_, y_, x_):
        return {"blk": 2 * z_ + y_, "enc": x_}

    def remote(src, dst, s, r, device):
        return pltpu.make_async_remote_copy(
            src_ref=src, dst_ref=dst, send_sem=s, recv_sem=r, device_id=device, device_id_type=MESH
        )

    sign = (1, -1)

    def layer(direction, distance):
        return (z - sign[direction] * distance + LAYERS) % LAYERS

    def onward(direction):
        return at((z + sign[direction] + LAYERS) % LAYERS, y, x)

    def unit(buf, s, r, direction, distance, order, sem):
        slot = 2 * layer(direction, distance) + (y + order) % 2
        return remote(
            buf.at[slot], buf.at[slot],
            s.at[direction, sem, order], r.at[direction, sem, order], onward(direction),
        )

    ring_a = (img_a, za_s, za_r)
    ring_b = (img_b, zb_s, zb_r)

    def send_own(ring, order):
        for direction in range(2):
            unit(*ring, direction, 0, order, 0).start()

    def ring_event(ring, distance, order):
        for direction in range(2):
            if distance == 4 and order != direction:
                continue
            unit(*ring, direction, distance, order, distance - 1).wait_recv()
            if distance < 3 or (distance == 3 and order == direction):
                unit(*ring, direction, distance, order, distance).start()

    def ring_last(ring):
        ring_event(ring, 4, 0)
        ring_event(ring, 4, 1)

    def ring_sent(ring):
        for direction in range(2):
            for distance in range(4):
                for order in range(2):
                    if distance < 3 or order == direction:
                        unit(*ring, direction, distance, order, distance).wait_send()

    def text_unit(direction, distance, sem):
        chunk = 2 * layer(direction, distance) + y
        return remote(
            text.at[chunk], text.at[chunk],
            tz_s.at[direction, sem], tz_r.at[direction, sem], onward(direction),
        )

    def text_across(chunk_layer, y_):
        chunk = 2 * chunk_layer + y_
        return remote(
            text.at[chunk], text.at[chunk], ty_s.at[chunk_layer], ty_r.at[chunk_layer],
            {"blk": partner},
        )

    def text_event(distance):
        for direction in range(2):
            if distance == 4 and direction == 1:
                continue
            text_unit(direction, distance, distance - 1).wait_recv()
            if distance < 3 or (distance == 3 and direction == 0):
                text_unit(direction, distance, distance).start()
            text_across(layer(direction, distance), y).start()

    def peer(step):
        return (x + step) % ENC

    def sq_copy(step):
        return remote(sq_ref, sq.at[x], sq_s.at[step], sq_r.at[x], at(z, y, peer(step)))

    def cq_copy(flip, step):
        return remote(
            cq_ref, cq.at[x, y], cq_s.at[flip, step], cq_r.at[x, y],
            at(z, (y + flip) % 2, peer(step)),
        )

    def part(half, which):
        size = (FIRST, SECOND)[which]
        start = pl.multiple_of(half * HALF + which * FIRST, 16)
        return img_ref.at[:, pl.ds(start, size), :]

    def half_copy(buf, which):
        slot = 2 * z + y
        return remote(
            part(1 - y, which), buf.at[slot], y_s.at[which], y_r.at[which], {"blk": partner}
        )

    def half_wait(buf, which):
        slot = 2 * z + 1 - y
        remote(
            part(1 - y, which), buf.at[slot], y_s.at[which], y_r.at[which], {"blk": partner}
        ).wait_recv()

    seen_copy = remote(seen.at[y], seen.at[y], y_s.at[2], y_r.at[2], {"blk": partner})

    own = 2 * z + y
    loads = [
        pltpu.make_async_copy(src, dst, load_sem.at[k])
        for k, (src, dst) in enumerate(
            (
                (text_ref, text.at[own]),
                (part(y, 0), img_a.at[own]),
                (part(y, 1), img_b.at[own]),
                (sq_ref, sq.at[x]),
                (cq_ref, cq.at[x, y]),
            )
        )
    ]
    for load in loads:
        load.start()

    barrier = pltpu.get_barrier_semaphore()
    for flip in range(2):
        for step in range(ENC):
            if flip or step:
                pl.semaphore_signal(
                    barrier, inc=1, device_id=at(z, (y + flip) % 2, peer(step)), device_id_type=MESH
                )
    for direction in range(2):
        pl.semaphore_signal(barrier, inc=1, device_id=onward(direction), device_id_type=MESH)

    seen[y] = jnp.zeros((8, 128), jnp.int32)
    seen[y, 0:4, 0:16] = seen_ref[...]

    pl.semaphore_wait(barrier, 9)

    half_copy(img_a, 0).start()
    for load in loads:
        load.wait()
    for direction in range(2):
        text_unit(direction, 0, 0).start()
    send_own(ring_a, 0)
    for step in (1, 3, 2):
        sq_copy(step).start()
    text_event(1)
    half_wait(img_a, 0)
    send_own(ring_a, 1)
    text_across(z, y).start()
    seen_copy.start()
    half_copy(img_b, 1).start()
    text_event(2)
    ring_event(ring_a, 1, 0)
    cq_copy(1, 0).start()
    text_event(3)
    text_event(4)
    ring_event(ring_a, 1, 1)
    cq_copy(0, 1).start()
    cq_copy(0, 3).start()
    ring_event(ring_a, 2, 0)
    cq_copy(1, 1).start()
    for k in range(LAYERS):
        text_across(k, 1 - y).wait_recv()
    for step in (1, 2, 3):
        other = peer(step)
        remote(sq.at[other], sq.at[other], sq_s.at[step], sq_r.at[other], at(z, y, other)).wait_recv()

    diagonal = lax.broadcasted_iota(jnp.int32, (BLOCK, BLOCK), 0) == lax.broadcasted_iota(
        jnp.int32, (BLOCK, BLOCK), 1
    )

    def pair(ref, rows):
        return jnp.concatenate([ref[rows, 0:HEAD], ref[rows, HEAD : 2 * HEAD]], axis=0)

    def put(part, lse, block, t, weighted, total, level):
        for k in range(2):
            mine = slice(k * BLOCK, (k + 1) * BLOCK)
            part[block, t, :, k * HEAD : (k + 1) * HEAD] = weighted[mine].astype(BF)
            square = jnp.where(diagonal, level[mine], 0.0)
            lse[block, t, k : k + 1, :] = jnp.sum(square, axis=0, keepdims=True)
            square = jnp.where(diagonal, total[mine], 0.0)
            lse[block, t, 2 + k : 3 + k, :] = jnp.sum(square, axis=0, keepdims=True)

    def s_copies(rb, step):
        t = peer(step)
        device = at(z, y, t)
        return (
            remote(s_part.at[rb, t], s_got.at[x, rb], so_s.at[rb, step], so_r.at[x, rb], device),
            remote(s_lse.at[rb, t], s_got_lse.at[x, rb], sl_s.at[rb, step], sl_r.at[x, rb], device),
        )

    def self_step(rb):
        rows = pl.ds(pl.multiple_of(rb * BLOCK, BLOCK), BLOCK)
        keys = text[:, :, 0:HEAD].reshape(16 * BLOCK, HEAD)
        values = text[:, :, HEAD:].reshape(16 * BLOCK, HEAD)
        row = lax.broadcasted_iota(jnp.int32, (TILE, 1), 0) % BLOCK
        inside = jnp.where(x < rb, BLOCK, jnp.where(x == rb, row + 1, 0))
        limit = blk * BLOCK + inside
        for t in range(ENC):
            s = dot_t(pair(sq.at[t], rows), keys)
            index = lax.broadcasted_iota(jnp.int32, s.shape, 1)
            s = jnp.where(index < limit, s, NEG)
            m = jnp.max(s, axis=1, keepdims=True) * EXP_SCALE
            pv = weigh(jnp.exp2(s * EXP_SCALE - m), values)
            put(s_part, s_lse, rb, t, pv[:, :HEAD], pv[:, HEAD:], m)
        s_got[x, rb] = s_part[rb, x]
        s_got_lse[x, rb] = s_lse[rb, x]

    def self_loop(i, carry):
        @pl.when(i == 0)
        def _():
            ring_event(ring_a, 2, 1)
            cq_copy(1, 3).start()

        @pl.when(i == 2)
        def _():
            ring_event(ring_a, 3, 0)
            send_own(ring_b, 0)
            cq_copy(0, 2).start()

        @pl.when(i == 3)
        def _():
            ring_event(ring_a, 3, 1)
            half_wait(img_b, 1)
            send_own(ring_b, 1)
            cq_copy(1, 2).start()

        self_step(i)
        return carry

    lax.fori_loop(0, 4, self_loop, 0)
    ring_last(ring_a)

    remote(seen.at[1 - y], seen.at[1 - y], y_s.at[2], y_r.at[2], {"blk": partner}).wait_recv()
    to_scalar = pltpu.make_async_copy(seen, seen_sm, local_sem)
    to_scalar.start()
    to_scalar.wait()

    def choose(b, carry):
        latest = jnp.int32(0)
        earlier = jnp.int32(0)
        count = jnp.int32(0)
        for i in range(16):
            flag = seen_sm[b // 4, b % 4, i] > 0
            slot = owner_ref[i]
            earlier = jnp.where(jnp.logical_and(flag, count == 0), slot, earlier)
            latest = jnp.where(flag, slot, latest)
            count = count + jnp.where(flag, 1, 0)
        pick[b, 0] = latest
        pick[b, 1] = earlier
        bias[b] = jnp.where(count > 1, 0.0, NEG)
        return carry

    lax.fori_loop(0, 8, choose, 0)
    for flip in range(2):
        for step in range(ENC):
            if flip or step:
                ox, oy = peer(step), (y + flip) % 2
                remote(
                    cq.at[ox, oy], cq.at[ox, oy], cq_s.at[flip, step], cq_r.at[ox, oy], at(z, oy, ox)
                ).wait_recv()

    def first_step(i):
        chunk, rb = i % 2, i // 2
        b = chunk * 4 + rb
        rows = pl.ds(pl.multiple_of(rb * BLOCK, BLOCK), BLOCK)
        one, two, off = pick[b, 0], pick[b, 1], bias[b]
        for t in range(ENC):
            q = pair(cq.at[t, chunk], rows)
            s1 = dot_t(q, img_a[one, 0])
            s2 = dot_t(q, img_a[two, 0])
            m = jnp.maximum(
                jnp.max(s1, axis=1, keepdims=True) * EXP_SCALE,
                jnp.max(s2, axis=1, keepdims=True) * EXP_SCALE + off,
            )
            pv = weigh(jnp.exp2(s1 * EXP_SCALE - m), img_a[one, 1])
            pv = pv + weigh(jnp.exp2(s2 * EXP_SCALE - (m - off)), img_a[two, 1])
            acc[i, t] = pv[:, :HEAD]
            tot[i, t] = pv[:, HEAD:]
            top[i, t] = m

    def first_loop(i, carry):
        for k in range(5):

            @pl.when(i == 1 + k)
            def _():
                ring_event(ring_b, 1 + k // 2, k % 2)
                if k < 4:
                    for step in (1, 3, 2):
                        for copy in s_copies(k, step):
                            copy.start()

        first_step(i)
        return carry

    lax.fori_loop(0, 8, first_loop, 0)

    def store(rows, out, block, sem):
        place = pl.ds(pl.multiple_of(block * BLOCK, BLOCK), BLOCK)
        return pltpu.make_async_copy(rows.at[block], out.at[place, :], store_sem.at[sem])

    def combine(got, got_lse, sources, block, rows):
        stats = [got_lse[k, block] for k in range(sources)]
        levels = [stat[0:2] for stat in stats]
        high = functools.reduce(jnp.maximum, levels)
        shares = [jnp.exp2(level - high) for level in levels]
        total = functools.reduce(jnp.add, [s * stat[2:4] for s, stat in zip(shares, stats)])
        shares = [share / total for share in shares]
        for hh in range(2):
            lanes = slice(hh * HEAD, (hh + 1) * HEAD)
            mixed = jnp.zeros((BLOCK, HEAD), F32)
            for k in range(sources):
                line = jnp.broadcast_to(shares[k][hh : hh + 1], (BLOCK, BLOCK))
                share = jnp.sum(jnp.where(diagonal, line, 0.0), axis=1, keepdims=True)
                mixed = mixed + got[k, block, :, lanes].astype(F32) * share
            rows[block, :, lanes] = mixed.astype(BF)

    def self_combine(rb, carry):
        for step in (1, 2, 3):
            o = peer(step)
            device = at(z, y, o)
            remote(s_part.at[rb, o], s_got.at[o, rb], so_s.at[rb, step], so_r.at[o, rb], device).wait_recv()
            remote(s_lse.at[rb, o], s_got_lse.at[o, rb], sl_s.at[rb, step], sl_r.at[o, rb], device).wait_recv()
        combine(s_got, s_got_lse, 4, rb, self_rows)
        store(self_rows, self_out, rb, rb).start()
        return carry

    lax.fori_loop(0, 4, self_combine, 0)
    ring_event(ring_b, 3, 1)
    ring_last(ring_b)

    def c_copies(b, chunk, rb, step):
        t = peer(step)
        device = at(z, chunk, t)
        source = 2 * x + y
        return (
            remote(c_part.at[b, t], c_got.at[source, rb], co_s.at[b, step], co_r.at[source, rb], device),
            remote(c_lse.at[b, t], c_got_lse.at[source, rb], cl_s.at[b, step], cl_r.at[source, rb], device),
        )

    valid = jnp.where(y == 0, SECOND, LAST_VALID)

    def second_loop(i, carry):
        chunk, rb = i % 2, i // 2
        b = chunk * 4 + rb
        rows = pl.ds(pl.multiple_of(rb * BLOCK, BLOCK), BLOCK)
        one, two, off = pick[b, 0], pick[b, 1], bias[b]
        keep = lax.broadcasted_iota(jnp.int32, (TILE, SECOND - WHOLE), 1) < valid - WHOLE

        def scores(q, slot):
            s = dot_t(q, img_b[slot, 0])
            return jnp.concatenate([s[:, :WHOLE], jnp.where(keep, s[:, WHOLE:], NEG)], axis=1)

        for t in range(ENC):
            q = pair(cq.at[t, chunk], rows)
            s1 = scores(q, one)
            s2 = scores(q, two)
            before = top[i, t]
            m = jnp.maximum(
                jnp.max(s1, axis=1, keepdims=True) * EXP_SCALE,
                jnp.max(s2, axis=1, keepdims=True) * EXP_SCALE + off,
            )
            m = jnp.maximum(m, before)
            fade = jnp.exp2(before - m)
            pv = weigh(jnp.exp2(s1 * EXP_SCALE - m), img_b[one, 1])
            pv = pv + weigh(jnp.exp2(s2 * EXP_SCALE - (m - off)), img_b[two, 1])
            put(c_part, c_lse, b, t, acc[i, t] * fade + pv[:, :HEAD], tot[i, t] * fade + pv[:, HEAD:], m)

        for step in (2, 1, 3):
            for copy in c_copies(b, chunk, rb, step):
                copy.start()

        @pl.when(chunk == y)
        def _():
            c_got[2 * x + y, rb] = c_part[b, x]
            c_got_lse[2 * x + y, rb] = c_lse[b, x]

        @pl.when(chunk != y)
        def _():
            for copy in c_copies(b, chunk, rb, 0):
                copy.start()

        return carry

    lax.fori_loop(0, 8, second_loop, 0)

    def cross_combine(rb, carry):
        for flip in range(2):
            for step in range(ENC):
                if flip or step:
                    ox, oy = peer(step), (y + flip) % 2
                    o = 2 * ox + oy
                    device = at(z, oy, ox)
                    remote(
                        c_part.at[rb, ox], c_got.at[o, rb], co_s.at[rb, step], co_r.at[o, rb], device
                    ).wait_recv()
                    remote(
                        c_lse.at[rb, ox], c_got_lse.at[o, rb], cl_s.at[rb, step], cl_r.at[o, rb], device
                    ).wait_recv()
        combine(c_got, c_got_lse, 8, rb, cross_rows)
        store(cross_rows, cross_out, rb, 4 + rb).start()
        return carry

    lax.fori_loop(0, 4, cross_combine, 0)

    ring_sent(ring_a)
    ring_sent(ring_b)
    for direction in range(2):
        for distance in range(4):
            if distance < 3 or direction == 0:
                text_unit(direction, distance, distance).wait_send()
    for k in range(LAYERS):
        text_across(k, y).wait_send()
    half_copy(img_a, 0).wait_send()
    half_copy(img_b, 1).wait_send()
    seen_copy.wait_send()
    for step in (1, 2, 3):
        sq_copy(step).wait_send()
    for flip in range(2):
        for step in range(ENC):
            if flip or step:
                cq_copy(flip, step).wait_send()

    def results_sent(rb, carry):
        for step in (1, 2, 3):
            for copy in s_copies(rb, step):
                copy.wait_send()
            for chunk in range(2):
                for copy in c_copies(chunk * 4 + rb, chunk, rb, step):
                    copy.wait_send()
        for copy in c_copies((1 - y) * 4 + rb, 1 - y, rb, 0):
            copy.wait_send()
        return carry

    lax.fori_loop(0, 4, results_sent, 0)
    for rb in range(4):
        store(self_rows, self_out, rb, rb).wait()
        store(cross_rows, cross_out, rb, 4 + rb).wait()


def per_device(self_query, text_kv, cross_query, image_kv, block_images, image_owner):
    quarter = lax.dynamic_slice_in_dim(text_kv, lax.axis_index("enc") * BLOCK, BLOCK, 0)
    quarter = quarter.reshape(BLOCK, 2 * HEAD)
    image = jnp.pad(image_kv[0], ((0, 0), (0, 2 * HALF - TOKENS), (0, 0)))
    vmem = pl.BlockSpec(memory_space=pltpu.VMEM)
    hbm = pl.BlockSpec(memory_space=pl.ANY)
    smem = pl.BlockSpec(memory_space=pltpu.SMEM)
    dma = pltpu.SemaphoreType.DMA
    out = jax.ShapeDtypeStruct((ROWS, 2 * HEAD), BF)
    return pl.pallas_call(
        kernel,
        out_shape=(out, out),
        in_specs=[hbm, hbm, hbm, hbm, vmem, smem],
        out_specs=(hbm, hbm),
        scratch_shapes=[
            pltpu.VMEM((16, 2, FIRST, HEAD), BF),
            pltpu.VMEM((16, 2, SECOND, HEAD), BF),
            pltpu.VMEM((16, BLOCK, 2 * HEAD), BF),
            pltpu.VMEM((ENC, ROWS, 2 * HEAD), BF),
            pltpu.VMEM((ENC, 2, ROWS, 2 * HEAD), BF),
            pltpu.VMEM((2, 8, 128), jnp.int32),
            pltpu.SMEM((2, 8, 128), jnp.int32),
            pltpu.SMEM((8, 2), jnp.int32),
            pltpu.SMEM((8,), F32),
            pltpu.VMEM((8, ENC, TILE, HEAD), F32),
            pltpu.VMEM((8, ENC, TILE, HEAD), F32),
            pltpu.VMEM((8, ENC, TILE, 1), F32),
            pltpu.VMEM((4, ENC, BLOCK, 2 * HEAD), BF),
            pltpu.VMEM((4, ENC, 8, HEAD), F32),
            pltpu.VMEM((ENC, 4, BLOCK, 2 * HEAD), BF),
            pltpu.VMEM((ENC, 4, 8, HEAD), F32),
            pltpu.VMEM((8, ENC, BLOCK, 2 * HEAD), BF),
            pltpu.VMEM((8, ENC, 8, HEAD), F32),
            pltpu.VMEM((8, 4, BLOCK, 2 * HEAD), BF),
            pltpu.VMEM((8, 4, 8, HEAD), F32),
            dma((2, 4, 2)), dma((2, 4, 2)), dma((2, 4, 2)), dma((2, 4, 2)),
            dma((2, 4)), dma((2, 4)), dma((LAYERS,)), dma((LAYERS,)),
            dma((3,)), dma((3,)),
            dma((ENC,)), dma((ENC,)), dma((2, ENC)), dma((ENC, 2)),
            dma((4, ENC)), dma((ENC, 4)), dma((4, ENC)), dma((ENC, 4)),
            dma((8, ENC)), dma((8, 4)), dma((8, ENC)), dma((8, 4)),
            dma, dma((5,)), dma((8,)),
            pltpu.VMEM((4, BLOCK, 2 * HEAD), BF),
            pltpu.VMEM((4, BLOCK, 2 * HEAD), BF),
        ],
        compiler_params=pltpu.CompilerParams(
            collective_id=0, has_side_effects=True, vmem_limit_bytes=60 * 2**20
        ),
        cost_estimate=pl.CostEstimate(
            flops=512 * 22_000_000, bytes_accessed=8_000_000, transcendentals=22_000_000
        ),
    )(self_query, quarter, cross_query, image, block_images, image_owner)


def solution(mesh):
    spread = P("blk", ("tp", "enc"))
    return jax.shard_map(
        per_device,
        mesh=mesh,
        in_specs=(spread, P("blk", None, "tp"), spread, P("blk", None, "enc", "tp"), P("blk", None), P()),
        out_specs=(spread, spread),
        check_vma=False,
    )
```

```python
import functools
import math

import jax
import jax.numpy as jnp
from jax import lax
from jax.experimental import pallas as pl
from jax.experimental.pallas import tpu as pltpu
from jax.sharding import PartitionSpec as P

MESH = pl.DeviceIdType.MESH
BF = jnp.bfloat16
F32 = jnp.float32
LAYERS = 8
ENC = 4
HEAD = 128
BLOCK = 128
ROWS = 512
TOKENS = 1601
HALF = 816
SIZES = (512, 304)
STARTS = (0, 512)
LAST_VALID = TOKENS - HALF - STARTS[1]
NEG = -1e30
EXP_SCALE = math.log2(math.e) / math.sqrt(HEAD)
TILE = 256


def dot_t(a, b):
    return lax.dot_general(a, b, (((1,), (1,)), ((), ())), preferred_element_type=F32)


def weigh(p, v):
    ones = jnp.ones(v.shape, BF)
    return jnp.dot(p.astype(BF), jnp.concatenate([v, ones], axis=1), preferred_element_type=F32)


def kernel(
    sq_ref, text_ref, cq_ref, img_ref, seen_ref, owner_ref,
    out_ref,
    img_a, img_b, raw, raw_text, stage_a, stage_b, text, sq, cq, seen, seen_sm, pick, bias,
    acc, tot, top,
    s_part, s_lse, s_got, s_got_lse,
    c_part, c_lse, c_got, c_got_lse,
    za_s, za_r, zb_s, zb_r, tz_s, tz_r, ty_s, ty_r, y_s, y_r,
    sq_s, sq_r, cq_s, cq_r, so_s, so_r, sl_s, sl_r, co_s, co_r, cl_s, cl_r, local_sem, load_sem, store_sem, self_rows, cross_rows,
):
    blk = lax.axis_index("blk")
    x = lax.axis_index("enc")
    z = blk // 2
    y = blk % 2
    partner = 2 * z + 1 - y

    def at(z_, y_, x_):
        return {"blk": 2 * z_ + y_, "enc": x_}

    def remote(src, dst, s, r, device):
        return pltpu.make_async_remote_copy(
            src_ref=src, dst_ref=dst, send_sem=s, recv_sem=r, device_id=device, device_id_type=MESH
        )

    sign = (1, -1)

    def layer(direction, distance):
        return (z - sign[direction] * distance + LAYERS) % LAYERS

    def onward(direction):
        return at((z + sign[direction] + LAYERS) % LAYERS, y, x)

    def unit(buf, s, r, direction, distance, order, sem):
        slot = 2 * layer(direction, distance) + (y + order) % 2
        return remote(
            buf.at[slot], buf.at[slot],
            s.at[direction, sem, order], r.at[direction, sem, order], onward(direction),
        )

    ring_a = (img_a, za_s, za_r)
    ring_b = (img_b, zb_s, zb_r)

    def send_own(ring, order):
        for direction in range(2):
            unit(*ring, direction, 0, order, 0).start()

    def ring_event(ring, distance, order):
        for direction in range(2):
            if distance == 4 and order != direction:
                continue
            unit(*ring, direction, distance, order, distance - 1).wait_recv()
            if distance < 3 or (distance == 3 and order == direction):
                unit(*ring, direction, distance, order, distance).start()

    def ring_last(ring):
        ring_event(ring, 4, 0)
        ring_event(ring, 4, 1)

    def ring_sent(ring):
        for direction in range(2):
            for distance in range(4):
                for order in range(2):
                    if distance < 3 or order == direction:
                        unit(*ring, direction, distance, order, distance).wait_send()

    def text_unit(direction, distance, sem):
        chunk = 2 * layer(direction, distance) + y
        return remote(
            text.at[chunk], text.at[chunk],
            tz_s.at[direction, sem], tz_r.at[direction, sem], onward(direction),
        )

    def text_across(chunk_layer, y_):
        chunk = 2 * chunk_layer + y_
        return remote(
            text.at[chunk], text.at[chunk], ty_s.at[chunk_layer], ty_r.at[chunk_layer],
            {"blk": partner},
        )

    def text_event(distance):
        for direction in range(2):
            if distance == 4 and direction == 1:
                continue
            text_unit(direction, distance, distance - 1).wait_recv()
            if distance < 3 or (distance == 3 and direction == 0):
                text_unit(direction, distance, distance).start()
            text_across(layer(direction, distance), y).start()

    def peer(step):
        return (x + step) % ENC

    def sq_copy(step):
        return remote(sq_ref, sq.at[x], sq_s.at[step], sq_r.at[x], at(z, y, peer(step)))

    def cq_copy(flip, step):
        return remote(
            cq_ref, cq.at[x, y], cq_s.at[flip, step], cq_r.at[x, y],
            at(z, (y + flip) % 2, peer(step)),
        )

    stages = ((stage_a, img_a), (stage_b, img_b))

    def half_copy(which, slot):
        stage, buf = stages[which]
        return remote(stage, buf.at[slot], y_s.at[which], y_r.at[which], {"blk": partner})

    def half_send(which):
        return half_copy(which, 2 * z + y)

    def half_wait(which):
        half_copy(which, 2 * z + 1 - y).wait_recv()

    seen_copy = remote(seen.at[y], seen.at[y], y_s.at[2], y_r.at[2], {"blk": partner})

    own = 2 * z + y
    quarter = pl.ds(pl.multiple_of(x * BLOCK, BLOCK), BLOCK)
    loads = [
        pltpu.make_async_copy(src, dst, load_sem.at[k])
        for k, (src, dst) in enumerate(
            (
                (img_ref, raw.at[pl.ds(0, TOKENS)]),
                (text_ref.at[quarter], raw_text),
                (sq_ref, sq.at[x]),
                (cq_ref, cq.at[x, y]),
            )
        )
    ]
    for load in loads:
        load.start()
    raw[TOKENS:] = jnp.zeros((2 * HALF - TOKENS, 2, HEAD), BF)

    barrier = pltpu.get_barrier_semaphore()
    for flip in range(2):
        for step in range(ENC):
            if flip or step:
                pl.semaphore_signal(
                    barrier, inc=1, device_id=at(z, (y + flip) % 2, peer(step)), device_id_type=MESH
                )
    for direction in range(2):
        pl.semaphore_signal(barrier, inc=1, device_id=onward(direction), device_id_type=MESH)

    for load in loads:
        load.wait()
    for kv in range(2):
        text[own, :, kv * HEAD : (kv + 1) * HEAD] = raw_text[:, kv, :]
        for which, (stage, buf) in enumerate(stages):
            size = SIZES[which]
            buf[own, kv] = raw[pl.ds(y * HALF + STARTS[which], size), kv, :]
            stage[kv] = raw[pl.ds((1 - y) * HALF + STARTS[which], size), kv, :]
    seen[y] = jnp.zeros((8, 128), jnp.int32)
    seen[y, 0:4, 0:16] = seen_ref[...]

    pl.semaphore_wait(barrier, 9)

    half_send(0).start()
    for direction in range(2):
        text_unit(direction, 0, 0).start()
    send_own(ring_a, 0)
    for step in (1, 3, 2):
        sq_copy(step).start()
    text_event(1)
    half_wait(0)
    send_own(ring_a, 1)
    text_across(z, y).start()
    seen_copy.start()
    half_send(1).start()
    text_event(2)
    ring_event(ring_a, 1, 0)
    cq_copy(1, 0).start()
    text_event(3)
    text_event(4)
    ring_event(ring_a, 1, 1)
    cq_copy(0, 1).start()
    cq_copy(0, 3).start()
    ring_event(ring_a, 2, 0)
    cq_copy(1, 1).start()
    for k in range(LAYERS):
        text_across(k, 1 - y).wait_recv()
    for step in (1, 2, 3):
        other = peer(step)
        remote(sq.at[other], sq.at[other], sq_s.at[step], sq_r.at[other], at(z, y, other)).wait_recv()

    diagonal = lax.broadcasted_iota(jnp.int32, (BLOCK, BLOCK), 0) == lax.broadcasted_iota(
        jnp.int32, (BLOCK, BLOCK), 1
    )

    def pair(ref, rows):
        return jnp.concatenate([ref[rows, 0:HEAD], ref[rows, HEAD : 2 * HEAD]], axis=0)

    def put(part, lse, block, t, weighted, total, level):
        for k in range(2):
            mine = slice(k * BLOCK, (k + 1) * BLOCK)
            part[block, t, :, k * HEAD : (k + 1) * HEAD] = weighted[mine].astype(BF)
            square = jnp.where(diagonal, level[mine], 0.0)
            lse[block, t, k : k + 1, :] = jnp.sum(square, axis=0, keepdims=True)
            square = jnp.where(diagonal, total[mine], 0.0)
            lse[block, t, 2 + k : 3 + k, :] = jnp.sum(square, axis=0, keepdims=True)

    def s_copies(rb, step):
        t = peer(step)
        device = at(z, y, t)
        return (
            remote(s_part.at[rb, t], s_got.at[x, rb], so_s.at[rb, step], so_r.at[x, rb], device),
            remote(s_lse.at[rb, t], s_got_lse.at[x, rb], sl_s.at[rb, step], sl_r.at[x, rb], device),
        )

    def self_step(rb):
        rows = pl.ds(pl.multiple_of(rb * BLOCK, BLOCK), BLOCK)
        keys = text[:, :, 0:HEAD].reshape(16 * BLOCK, HEAD)
        values = text[:, :, HEAD:].reshape(16 * BLOCK, HEAD)
        row = lax.broadcasted_iota(jnp.int32, (TILE, 1), 0) % BLOCK
        inside = jnp.where(x < rb, BLOCK, jnp.where(x == rb, row + 1, 0))
        limit = blk * BLOCK + inside
        index = lax.broadcasted_iota(jnp.int32, (TILE, 16 * BLOCK), 1)
        scores = [jnp.where(index < limit, dot_t(pair(sq.at[t], rows), keys), NEG) for t in range(ENC)]
        tops = [jnp.max(s, axis=1, keepdims=True) * EXP_SCALE for s in scores]
        mixed = [weigh(jnp.exp2(s * EXP_SCALE - m), values) for s, m in zip(scores, tops)]
        for t in range(ENC):
            put(s_part, s_lse, rb, t, mixed[t][:, :HEAD], mixed[t][:, HEAD:], tops[t])
        s_got[x, rb] = s_part[rb, x]
        s_got_lse[x, rb] = s_lse[rb, x]

    def self_loop(i, carry):
        @pl.when(i == 0)
        def _():
            ring_event(ring_a, 2, 1)
            cq_copy(1, 3).start()

        @pl.when(i == 2)
        def _():
            ring_event(ring_a, 3, 0)
            send_own(ring_b, 0)
            cq_copy(0, 2).start()

        @pl.when(i == 3)
        def _():
            ring_event(ring_a, 3, 1)
            half_wait(1)
            send_own(ring_b, 1)
            cq_copy(1, 2).start()

        self_step(i)
        return carry

    lax.fori_loop(0, 4, self_loop, 0)
    ring_last(ring_a)

    remote(seen.at[1 - y], seen.at[1 - y], y_s.at[2], y_r.at[2], {"blk": partner}).wait_recv()
    to_scalar = pltpu.make_async_copy(seen, seen_sm, local_sem)
    to_scalar.start()
    to_scalar.wait()

    def choose(b, carry):
        latest = jnp.int32(0)
        earlier = jnp.int32(0)
        count = jnp.int32(0)
        for i in range(16):
            flag = seen_sm[b // 4, b % 4, i] > 0
            slot = owner_ref[i]
            earlier = jnp.where(jnp.logical_and(flag, count == 0), slot, earlier)
            latest = jnp.where(flag, slot, latest)
            count = count + jnp.where(flag, 1, 0)
        pick[b, 0] = latest
        pick[b, 1] = earlier
        bias[b] = jnp.where(count > 1, 0.0, NEG)
        return carry

    lax.fori_loop(0, 8, choose, 0)
    for flip in range(2):
        for step in range(ENC):
            if flip or step:
                ox, oy = peer(step), (y + flip) % 2
                remote(
                    cq.at[ox, oy], cq.at[ox, oy], cq_s.at[flip, step], cq_r.at[ox, oy], at(z, oy, ox)
                ).wait_recv()

    def block_of(i):
        chunk, rb = i % 2, i // 2
        b = chunk * 4 + rb
        rows = pl.ds(pl.multiple_of(rb * BLOCK, BLOCK), BLOCK)
        return chunk, rb, b, rows, pick[b, 0], pick[b, 1], bias[b]

    def tops_of(scores):
        return [
            jnp.maximum(jnp.max(s1, axis=1, keepdims=True), jnp.max(s2, axis=1, keepdims=True))
            for s1, s2 in scores
        ]

    def mix(scores, tops, v1, v2):
        return [
            weigh(jnp.exp2(s1 - m), v1) + weigh(jnp.exp2(s2 - m), v2)
            for (s1, s2), m in zip(scores, tops)
        ]

    def first_step(i):
        chunk, rb, b, rows, one, two, off = block_of(i)
        k1, k2, v1, v2 = img_a[one, 0], img_a[two, 0], img_a[one, 1], img_a[two, 1]
        queries = [pair(cq.at[t, chunk], rows) for t in range(ENC)]
        scores = [(dot_t(q, k1) * EXP_SCALE, dot_t(q, k2) * EXP_SCALE + off) for q in queries]
        tops = tops_of(scores)
        mixed = mix(scores, tops, v1, v2)
        for t in range(ENC):
            acc[i, t] = mixed[t][:, :HEAD]
            tot[i, t] = mixed[t][:, HEAD:]
            top[i, t] = tops[t]

    def pass_event(k):
        if k < 6:
            ring_event(ring_b, 1 + k // 2, k % 2)
        else:
            ring_last(ring_b)

    def first_loop(i, carry):
        for k in range(7):

            @pl.when(i == k)
            def _():
                pass_event(k)
                if k < 4:
                    for step in (1, 3, 2):
                        for copy in s_copies(k, step):
                            copy.start()

        first_step(i)
        return carry

    lax.fori_loop(0, 8, first_loop, 0)

    def store(rows, which, block, sem):
        place = pl.ds(pl.multiple_of(block * BLOCK, BLOCK), BLOCK)
        return pltpu.make_async_copy(rows.at[block], out_ref.at[which, place, :], store_sem.at[sem])

    def combine(got, got_lse, sources, block, rows):
        stats = [got_lse[k, block] for k in range(sources)]
        levels = [stat[0:2] for stat in stats]
        high = functools.reduce(jnp.maximum, levels)
        shares = [jnp.exp2(level - high) for level in levels]
        total = functools.reduce(jnp.add, [s * stat[2:4] for s, stat in zip(shares, stats)])
        shares = [share / total for share in shares]
        for hh in range(2):
            lanes = slice(hh * HEAD, (hh + 1) * HEAD)
            mixed = jnp.zeros((BLOCK, HEAD), F32)
            for k in range(sources):
                line = jnp.broadcast_to(shares[k][hh : hh + 1], (BLOCK, BLOCK))
                share = jnp.sum(jnp.where(diagonal, line, 0.0), axis=1, keepdims=True)
                mixed = mixed + got[k, block, :, lanes].astype(F32) * share
            rows[block, :, lanes] = mixed.astype(BF)

    def self_combine(rb, carry):
        for step in (1, 2, 3):
            o = peer(step)
            device = at(z, y, o)
            remote(s_part.at[rb, o], s_got.at[o, rb], so_s.at[rb, step], so_r.at[o, rb], device).wait_recv()
            remote(s_lse.at[rb, o], s_got_lse.at[o, rb], sl_s.at[rb, step], sl_r.at[o, rb], device).wait_recv()
        combine(s_got, s_got_lse, 4, rb, self_rows)
        store(self_rows, 0, rb, rb).start()
        return carry

    lax.fori_loop(0, 4, self_combine, 0)

    def c_copies(b, chunk, rb, step):
        t = peer(step)
        device = at(z, chunk, t)
        source = 2 * x + y
        return (
            remote(c_part.at[b, t], c_got.at[source, rb], co_s.at[b, step], co_r.at[source, rb], device),
            remote(c_lse.at[b, t], c_got_lse.at[source, rb], cl_s.at[b, step], cl_r.at[source, rb], device),
        )

    valid = jnp.where(y == 0, SIZES[1], LAST_VALID)

    def last_loop(i, carry):
        chunk, rb, b, rows, one, two, off = block_of(i)
        bias_one = jnp.where(lax.broadcasted_iota(jnp.int32, (1, SIZES[1]), 1) < valid, 0.0, NEG)
        bias_two = bias_one + off
        before = [top[i, t] for t in range(ENC)]
        k1, k2, v1, v2 = img_b[one, 0], img_b[two, 0], img_b[one, 1], img_b[two, 1]
        queries = [pair(cq.at[t, chunk], rows) for t in range(ENC)]
        scores = [
            (dot_t(q, k1) * EXP_SCALE + bias_one, dot_t(q, k2) * EXP_SCALE + bias_two) for q in queries
        ]
        tops = [jnp.maximum(m, old) for m, old in zip(tops_of(scores), before)]
        mixed = mix(scores, tops, v1, v2)
        fades = [jnp.exp2(old - m) for old, m in zip(before, tops)]
        weighted = [acc[i, t] * fades[t] + mixed[t][:, :HEAD] for t in range(ENC)]
        totals = [tot[i, t] * fades[t] + mixed[t][:, HEAD:] for t in range(ENC)]
        for t in range(ENC):
            put(c_part, c_lse, b, t, weighted[t], totals[t], tops[t])

        for step in (2, 1, 3):
            for copy in c_copies(b, chunk, rb, step):
                copy.start()

        @pl.when(chunk == y)
        def _():
            c_got[2 * x + y, rb] = c_part[b, x]
            c_got_lse[2 * x + y, rb] = c_lse[b, x]

        @pl.when(chunk != y)
        def _():
            for copy in c_copies(b, chunk, rb, 0):
                copy.start()

        return carry

    lax.fori_loop(0, 8, last_loop, 0)

    def cross_combine(rb, carry):
        for flip in range(2):
            for step in range(ENC):
                if flip or step:
                    ox, oy = peer(step), (y + flip) % 2
                    o = 2 * ox + oy
                    device = at(z, oy, ox)
                    remote(
                        c_part.at[rb, ox], c_got.at[o, rb], co_s.at[rb, step], co_r.at[o, rb], device
                    ).wait_recv()
                    remote(
                        c_lse.at[rb, ox], c_got_lse.at[o, rb], cl_s.at[rb, step], cl_r.at[o, rb], device
                    ).wait_recv()
        combine(c_got, c_got_lse, 8, rb, cross_rows)
        store(cross_rows, 1, rb, 4 + rb).start()
        return carry

    lax.fori_loop(0, 4, cross_combine, 0)

    ring_sent(ring_a)
    ring_sent(ring_b)
    for direction in range(2):
        for distance in range(4):
            if distance < 3 or direction == 0:
                text_unit(direction, distance, distance).wait_send()
    for k in range(LAYERS):
        text_across(k, y).wait_send()
    for which in range(2):
        half_send(which).wait_send()
    seen_copy.wait_send()
    for step in (1, 2, 3):
        sq_copy(step).wait_send()
    for flip in range(2):
        for step in range(ENC):
            if flip or step:
                cq_copy(flip, step).wait_send()

    def results_sent(rb, carry):
        for step in (1, 2, 3):
            for copy in s_copies(rb, step):
                copy.wait_send()
            for chunk in range(2):
                for copy in c_copies(chunk * 4 + rb, chunk, rb, step):
                    copy.wait_send()
        for copy in c_copies((1 - y) * 4 + rb, 1 - y, rb, 0):
            copy.wait_send()
        return carry

    lax.fori_loop(0, 4, results_sent, 0)
    for rb in range(4):
        store(self_rows, 0, rb, rb).wait()
        store(cross_rows, 1, rb, 4 + rb).wait()


def per_device(self_query, text_kv, cross_query, image_kv, block_images, image_owner):
    image = jnp.swapaxes(image_kv[0], 0, 1)
    vmem = pl.BlockSpec(memory_space=pltpu.VMEM)
    hbm = pl.BlockSpec(memory_space=pl.ANY)
    smem = pl.BlockSpec(memory_space=pltpu.SMEM)
    dma = pltpu.SemaphoreType.DMA
    both = pl.pallas_call(
        kernel,
        out_shape=jax.ShapeDtypeStruct((2, ROWS, 2 * HEAD), BF),
        in_specs=[hbm, hbm, hbm, hbm, vmem, smem],
        out_specs=hbm,
        scratch_shapes=[
            *(pltpu.VMEM((16, 2, size, HEAD), BF) for size in SIZES),
            pltpu.VMEM((2 * HALF, 2, HEAD), BF),
            pltpu.VMEM((BLOCK, 2, HEAD), BF),
            *(pltpu.VMEM((2, size, HEAD), BF) for size in SIZES),
            pltpu.VMEM((16, BLOCK, 2 * HEAD), BF),
            pltpu.VMEM((ENC, ROWS, 2 * HEAD), BF),
            pltpu.VMEM((ENC, 2, ROWS, 2 * HEAD), BF),
            pltpu.VMEM((2, 8, 128), jnp.int32),
            pltpu.SMEM((2, 8, 128), jnp.int32),
            pltpu.SMEM((8, 2), jnp.int32),
            pltpu.SMEM((8,), F32),
            pltpu.VMEM((8, ENC, TILE, HEAD), F32),
            pltpu.VMEM((8, ENC, TILE, HEAD), F32),
            pltpu.VMEM((8, ENC, TILE, 1), F32),
            pltpu.VMEM((4, ENC, BLOCK, 2 * HEAD), BF),
            pltpu.VMEM((4, ENC, 8, HEAD), F32),
            pltpu.VMEM((ENC, 4, BLOCK, 2 * HEAD), BF),
            pltpu.VMEM((ENC, 4, 8, HEAD), F32),
            pltpu.VMEM((8, ENC, BLOCK, 2 * HEAD), BF),
            pltpu.VMEM((8, ENC, 8, HEAD), F32),
            pltpu.VMEM((8, 4, BLOCK, 2 * HEAD), BF),
            pltpu.VMEM((8, 4, 8, HEAD), F32),
            dma((2, 4, 2)), dma((2, 4, 2)), dma((2, 4, 2)), dma((2, 4, 2)),
            dma((2, 4)), dma((2, 4)), dma((LAYERS,)), dma((LAYERS,)),
            dma((3,)), dma((3,)),
            dma((ENC,)), dma((ENC,)), dma((2, ENC)), dma((ENC, 2)),
            dma((4, ENC)), dma((ENC, 4)), dma((4, ENC)), dma((ENC, 4)),
            dma((8, ENC)), dma((8, 4)), dma((8, ENC)), dma((8, 4)),
            dma, dma((4,)), dma((8,)),
            pltpu.VMEM((4, BLOCK, 2 * HEAD), BF),
            pltpu.VMEM((4, BLOCK, 2 * HEAD), BF),
        ],
        compiler_params=pltpu.CompilerParams(
            collective_id=0, has_side_effects=True, vmem_limit_bytes=60 * 2**20
        ),
        cost_estimate=pl.CostEstimate(
            flops=512 * 22_000_000, bytes_accessed=8_000_000, transcendentals=22_000_000
        ),
    )(self_query, text_kv, cross_query, image, block_images, image_owner)
    return both[0], both[1]


def solution(mesh):
    spread = P("blk", ("tp", "enc"))
    return jax.shard_map(
        per_device,
        mesh=mesh,
        in_specs=(spread, P("blk", None, "tp"), spread, P("blk", None, "enc", "tp"), P("blk", None), P()),
        out_specs=(spread, spread),
        check_vma=False,
    )
```

```python
import functools
import math

import jax
import jax.numpy as jnp
from jax import lax
from jax.experimental import pallas as pl
from jax.experimental.pallas import tpu as pltpu
from jax.sharding import PartitionSpec as P

MESH = pl.DeviceIdType.MESH
BF = jnp.bfloat16
F32 = jnp.float32
LAYERS = 8
ENC = 4
HEAD = 128
BLOCK = 128
ROWS = 512
TOKENS = 1601
HALF = 816
SIZES = (512, 304)
STARTS = (0, 512)
LAST_VALID = TOKENS - HALF - STARTS[1]
NEG = -1e30
EXP_SCALE = math.log2(math.e) / math.sqrt(HEAD)
TILE = 256


def dot_t(a, b):
    return lax.dot_general(a, b, (((1,), (1,)), ((), ())), preferred_element_type=F32)


def weigh(p, v):
    ones = jnp.ones(v.shape, BF)
    return jnp.dot(p.astype(BF), jnp.concatenate([v, ones], axis=1), preferred_element_type=F32)


def kernel(
    sq_ref, text_ref, cq_ref, img_ref, seen_ref, owner_ref,
    out_ref,
    img_a, img_b, raw, raw_text, stage_a, stage_b, text, sq, cq, seen, seen_sm, pick, bias,
    acc, tot, top,
    s_part, s_lse, s_got, s_got_lse,
    c_part, c_lse, c_got, c_got_lse,
    over, over_lse, side, side_lse, joint, joint_lse,
    za_s, za_r, zb_s, zb_r, tz_s, tz_r, ty_s, ty_r, y_s, y_r,
    sq_s, sq_r, cq_s, cq_r, so_s, so_r, sl_s, sl_r, co_s, co_r, cl_s, cl_r,
    oo_s, oo_r, ol_s, ol_r, do_s, do_r, dl_s, dl_r, jo_s, jo_r, jl_s, jl_r, local_sem, load_sem, store_sem, self_rows, cross_rows,
):
    blk = lax.axis_index("blk")
    x = lax.axis_index("enc")
    z = blk // 2
    y = blk % 2
    partner = 2 * z + 1 - y

    def at(z_, y_, x_):
        return {"blk": 2 * z_ + y_, "enc": x_}

    def remote(src, dst, s, r, device):
        return pltpu.make_async_remote_copy(
            src_ref=src, dst_ref=dst, send_sem=s, recv_sem=r, device_id=device, device_id_type=MESH
        )

    sign = (1, -1)

    def layer(direction, distance):
        return (z - sign[direction] * distance + LAYERS) % LAYERS

    def onward(direction):
        return at((z + sign[direction] + LAYERS) % LAYERS, y, x)

    def unit(buf, s, r, direction, distance, order, sem):
        slot = 2 * layer(direction, distance) + (y + order) % 2
        return remote(
            buf.at[slot], buf.at[slot],
            s.at[direction, sem, order], r.at[direction, sem, order], onward(direction),
        )

    ring_a = (img_a, za_s, za_r)
    ring_b = (img_b, zb_s, zb_r)

    def send_own(ring, order):
        for direction in range(2):
            unit(*ring, direction, 0, order, 0).start()

    def ring_event(ring, distance, order):
        for direction in range(2):
            if distance == 4 and order != direction:
                continue
            unit(*ring, direction, distance, order, distance - 1).wait_recv()
            if distance < 3 or (distance == 3 and order == direction):
                unit(*ring, direction, distance, order, distance).start()

    def ring_last(ring):
        ring_event(ring, 4, 0)
        ring_event(ring, 4, 1)

    def ring_sent(ring):
        for direction in range(2):
            for distance in range(4):
                for order in range(2):
                    if distance < 3 or order == direction:
                        unit(*ring, direction, distance, order, distance).wait_send()

    def text_unit(direction, distance, sem):
        chunk = 2 * layer(direction, distance) + y
        return remote(
            text.at[chunk], text.at[chunk],
            tz_s.at[direction, sem], tz_r.at[direction, sem], onward(direction),
        )

    def text_across(chunk_layer, y_):
        chunk = 2 * chunk_layer + y_
        return remote(
            text.at[chunk], text.at[chunk], ty_s.at[chunk_layer], ty_r.at[chunk_layer],
            {"blk": partner},
        )

    def text_event(distance):
        for direction in range(2):
            if distance == 4 and direction == 1:
                continue
            text_unit(direction, distance, distance - 1).wait_recv()
            if distance < 3 or (distance == 3 and direction == 0):
                text_unit(direction, distance, distance).start()
            text_across(layer(direction, distance), y).start()

    def peer(step):
        return (x + step) % ENC

    def sq_copy(step):
        return remote(sq_ref, sq.at[x], sq_s.at[step], sq_r.at[x], at(z, y, peer(step)))

    def cq_copy(flip, step):
        return remote(
            cq_ref, cq.at[x, y], cq_s.at[flip, step], cq_r.at[x, y],
            at(z, (y + flip) % 2, peer(step)),
        )

    stages = ((stage_a, img_a), (stage_b, img_b))

    def half_copy(which, slot):
        stage, buf = stages[which]
        return remote(stage, buf.at[slot], y_s.at[which], y_r.at[which], {"blk": partner})

    def half_send(which):
        return half_copy(which, 2 * z + y)

    def half_wait(which):
        half_copy(which, 2 * z + 1 - y).wait_recv()

    seen_copy = remote(seen.at[y], seen.at[y], y_s.at[2], y_r.at[2], {"blk": partner})

    own = 2 * z + y
    quarter = pl.ds(pl.multiple_of(x * BLOCK, BLOCK), BLOCK)
    loads = [
        pltpu.make_async_copy(src, dst, load_sem.at[k])
        for k, (src, dst) in enumerate(
            (
                (img_ref, raw.at[pl.ds(0, TOKENS)]),
                (text_ref.at[quarter], raw_text),
                (sq_ref, sq.at[x]),
                (cq_ref, cq.at[x, y]),
            )
        )
    ]
    for load in loads:
        load.start()
    raw[TOKENS:] = jnp.zeros((2 * HALF - TOKENS, 2, HEAD), BF)

    barrier = pltpu.get_barrier_semaphore()
    for flip in range(2):
        for step in range(ENC):
            if flip or step:
                pl.semaphore_signal(
                    barrier, inc=1, device_id=at(z, (y + flip) % 2, peer(step)), device_id_type=MESH
                )
    for direction in range(2):
        pl.semaphore_signal(barrier, inc=1, device_id=onward(direction), device_id_type=MESH)

    for load in loads:
        load.wait()
    for kv in range(2):
        text[own, :, kv * HEAD : (kv + 1) * HEAD] = raw_text[:, kv, :]
        for which, (stage, buf) in enumerate(stages):
            size = SIZES[which]
            buf[own, kv] = raw[pl.ds(y * HALF + STARTS[which], size), kv, :]
            stage[kv] = raw[pl.ds((1 - y) * HALF + STARTS[which], size), kv, :]
    seen[y] = jnp.zeros((8, 128), jnp.int32)
    seen[y, 0:4, 0:16] = seen_ref[...]

    pl.semaphore_wait(barrier, 9)

    half_send(0).start()
    for direction in range(2):
        text_unit(direction, 0, 0).start()
    send_own(ring_a, 0)
    for step in (1, 3, 2):
        sq_copy(step).start()
    text_event(1)
    half_wait(0)
    send_own(ring_a, 1)
    text_across(z, y).start()
    seen_copy.start()
    half_send(1).start()
    text_event(2)
    ring_event(ring_a, 1, 0)
    cq_copy(1, 0).start()
    text_event(3)
    text_event(4)
    ring_event(ring_a, 1, 1)
    cq_copy(0, 1).start()
    cq_copy(0, 3).start()
    ring_event(ring_a, 2, 0)
    cq_copy(1, 1).start()
    for k in range(LAYERS):
        text_across(k, 1 - y).wait_recv()
    for step in (1, 2, 3):
        other = peer(step)
        remote(sq.at[other], sq.at[other], sq_s.at[step], sq_r.at[other], at(z, y, other)).wait_recv()

    diagonal = lax.broadcasted_iota(jnp.int32, (BLOCK, BLOCK), 0) == lax.broadcasted_iota(
        jnp.int32, (BLOCK, BLOCK), 1
    )

    def pair(ref, rows):
        return jnp.concatenate([ref[rows, 0:HEAD], ref[rows, HEAD : 2 * HEAD]], axis=0)

    def put(part, lse, block, t, weighted, total, level):
        for k in range(2):
            mine = slice(k * BLOCK, (k + 1) * BLOCK)
            part[block, t, :, k * HEAD : (k + 1) * HEAD] = weighted[mine].astype(BF)
            square = jnp.where(diagonal, level[mine], 0.0)
            lse[block, t, k : k + 1, :] = jnp.sum(square, axis=0, keepdims=True)
            square = jnp.where(diagonal, total[mine], 0.0)
            lse[block, t, 2 + k : 3 + k, :] = jnp.sum(square, axis=0, keepdims=True)

    def s_copies(rb, step):
        t = peer(step)
        device = at(z, y, t)
        return (
            remote(s_part.at[rb, t], s_got.at[x, rb], so_s.at[rb, step], so_r.at[x, rb], device),
            remote(s_lse.at[rb, t], s_got_lse.at[x, rb], sl_s.at[rb, step], sl_r.at[x, rb], device),
        )

    def self_step(rb):
        rows = pl.ds(pl.multiple_of(rb * BLOCK, BLOCK), BLOCK)
        keys = text[:, :, 0:HEAD].reshape(16 * BLOCK, HEAD)
        values = text[:, :, HEAD:].reshape(16 * BLOCK, HEAD)
        row = lax.broadcasted_iota(jnp.int32, (TILE, 1), 0) % BLOCK
        inside = jnp.where(x < rb, BLOCK, jnp.where(x == rb, row + 1, 0))
        limit = blk * BLOCK + inside
        index = lax.broadcasted_iota(jnp.int32, (TILE, 16 * BLOCK), 1)
        scores = [jnp.where(index < limit, dot_t(pair(sq.at[t], rows), keys), NEG) for t in range(ENC)]
        tops = [jnp.max(s, axis=1, keepdims=True) * EXP_SCALE for s in scores]
        mixed = [weigh(jnp.exp2(s * EXP_SCALE - m), values) for s, m in zip(scores, tops)]
        for t in range(ENC):
            put(s_part, s_lse, rb, t, mixed[t][:, :HEAD], mixed[t][:, HEAD:], tops[t])
        s_got[x, rb] = s_part[rb, x]
        s_got_lse[x, rb] = s_lse[rb, x]

    def self_loop(i, carry):
        @pl.when(i == 0)
        def _():
            ring_event(ring_a, 2, 1)
            cq_copy(1, 3).start()

        @pl.when(i == 2)
        def _():
            ring_event(ring_a, 3, 0)
            send_own(ring_b, 0)
            cq_copy(0, 2).start()

        @pl.when(i == 3)
        def _():
            ring_event(ring_a, 3, 1)
            half_wait(1)
            send_own(ring_b, 1)
            cq_copy(1, 2).start()

        self_step(i)
        return carry

    lax.fori_loop(0, 4, self_loop, 0)
    ring_last(ring_a)

    remote(seen.at[1 - y], seen.at[1 - y], y_s.at[2], y_r.at[2], {"blk": partner}).wait_recv()
    to_scalar = pltpu.make_async_copy(seen, seen_sm, local_sem)
    to_scalar.start()
    to_scalar.wait()

    def choose(b, carry):
        latest = jnp.int32(0)
        earlier = jnp.int32(0)
        count = jnp.int32(0)
        for i in range(16):
            flag = seen_sm[b // 4, b % 4, i] > 0
            slot = owner_ref[i]
            earlier = jnp.where(jnp.logical_and(flag, count == 0), slot, earlier)
            latest = jnp.where(flag, slot, latest)
            count = count + jnp.where(flag, 1, 0)
        pick[b, 0] = latest
        pick[b, 1] = earlier
        bias[b] = jnp.where(count > 1, 0.0, NEG)
        return carry

    lax.fori_loop(0, 8, choose, 0)
    for flip in range(2):
        for step in range(ENC):
            if flip or step:
                ox, oy = peer(step), (y + flip) % 2
                remote(
                    cq.at[ox, oy], cq.at[ox, oy], cq_s.at[flip, step], cq_r.at[ox, oy], at(z, oy, ox)
                ).wait_recv()

    def block_of(i):
        chunk, rb = i % 2, i // 2
        b = chunk * 4 + rb
        rows = pl.ds(pl.multiple_of(rb * BLOCK, BLOCK), BLOCK)
        return chunk, rb, b, rows, pick[b, 0], pick[b, 1], bias[b]

    def tops_of(scores):
        return [
            jnp.maximum(jnp.max(s1, axis=1, keepdims=True), jnp.max(s2, axis=1, keepdims=True))
            for s1, s2 in scores
        ]

    def mix(scores, tops, v1, v2):
        return [
            weigh(jnp.exp2(s1 - m), v1) + weigh(jnp.exp2(s2 - m), v2)
            for (s1, s2), m in zip(scores, tops)
        ]

    def first_step(i):
        chunk, rb, b, rows, one, two, off = block_of(i)
        k1, k2, v1, v2 = img_a[one, 0], img_a[two, 0], img_a[one, 1], img_a[two, 1]
        queries = [pair(cq.at[t, chunk], rows) for t in range(ENC)]
        scores = [(dot_t(q, k1) * EXP_SCALE, dot_t(q, k2) * EXP_SCALE + off) for q in queries]
        tops = tops_of(scores)
        mixed = mix(scores, tops, v1, v2)
        for t in range(ENC):
            acc[i, t] = mixed[t][:, :HEAD]
            tot[i, t] = mixed[t][:, HEAD:]
            top[i, t] = tops[t]

    def pass_event(k):
        if k < 6:
            ring_event(ring_b, 1 + k // 2, k % 2)
        else:
            ring_last(ring_b)

    def first_loop(i, carry):
        for k in range(7):

            @pl.when(i == k + 1)
            def _():
                pass_event(k)
                if k < 4:
                    for step in (1, 3, 2):
                        for copy in s_copies(k, step):
                            copy.start()

        first_step(i)
        return carry

    lax.fori_loop(0, 8, first_loop, 0)

    def store(rows, which, block, sem):
        place = pl.ds(pl.multiple_of(block * BLOCK, BLOCK), BLOCK)
        return pltpu.make_async_copy(rows.at[block], out_ref.at[which, place, :], store_sem.at[sem])

    def blend(parts, stats, out, stat_out):
        stats = [stat[...] for stat in stats]
        levels = [stat[0:2] for stat in stats]
        high = functools.reduce(jnp.maximum, levels)
        shares = [jnp.exp2(level - high) for level in levels]
        total = functools.reduce(jnp.add, [s * stat[2:4] for s, stat in zip(shares, stats)])
        if stat_out is None:
            shares = [share / total for share in shares]
        else:
            stat_out[0:2, :] = high
            stat_out[2:4, :] = total
        for hh in range(2):
            lanes = slice(hh * HEAD, (hh + 1) * HEAD)
            mixed = jnp.zeros((BLOCK, HEAD), F32)
            for part, share in zip(parts, shares):
                line = jnp.broadcast_to(share[hh : hh + 1], (BLOCK, BLOCK))
                column = jnp.sum(jnp.where(diagonal, line, 0.0), axis=1, keepdims=True)
                mixed = mixed + part[:, lanes].astype(F32) * column
            out[:, lanes] = mixed.astype(BF)

    def combine(got, got_lse, sources, block, rows):
        blend(
            [got.at[k, block] for k in range(sources)],
            [got_lse.at[k, block] for k in range(sources)],
            rows.at[block],
            None,
        )

    def self_combine(rb, carry):
        for step in (1, 2, 3):
            o = peer(step)
            device = at(z, y, o)
            remote(s_part.at[rb, o], s_got.at[o, rb], so_s.at[rb, step], so_r.at[o, rb], device).wait_recv()
            remote(s_lse.at[rb, o], s_got_lse.at[o, rb], sl_s.at[rb, step], sl_r.at[o, rb], device).wait_recv()
        combine(s_got, s_got_lse, 4, rb, self_rows)
        store(self_rows, 0, rb, rb).start()
        return carry

    lax.fori_loop(0, 4, self_combine, 0)

    def pairs(src, src_lse, dst, dst_lse, so, ro, sl, rl, device):
        return (remote(src, dst, so, ro, device), remote(src_lse, dst_lse, sl, rl, device))

    def own_copies(rb, step, source):
        t, b = peer(step), 4 * y + rb
        return pairs(
            c_part.at[b, t], c_lse.at[b, t], c_got.at[source, rb], c_got_lse.at[source, rb],
            co_s.at[rb, step], co_r.at[source, rb], cl_s.at[rb, step], cl_r.at[source, rb], at(z, y, t),
        )

    def side_copies(rb, step, source):
        t, b = peer(step), 4 * (1 - y) + rb
        return pairs(
            c_part.at[b, t], c_lse.at[b, t], side.at[source, rb], side_lse.at[source, rb],
            do_s.at[rb, step], do_r.at[source, rb], dl_s.at[rb, step], dl_r.at[source, rb], at(z, y, t),
        )

    def over_copies(rb):
        b, k = 4 * (1 - y) + rb, rb - 2
        return pairs(
            c_part.at[b], c_lse.at[b], over.at[k], over_lse.at[k],
            oo_s.at[k], oo_r.at[k], ol_s.at[k], ol_r.at[k], {"blk": partner},
        )

    def joint_copies(rb):
        return pairs(
            joint.at[rb], joint_lse.at[rb], c_got.at[ENC, rb], c_got_lse.at[ENC, rb],
            jo_s.at[rb], jo_r.at[rb], jl_s.at[rb], jl_r.at[rb], {"blk": partner},
        )

    def start_own(rb):
        b = 4 * y + rb
        for step in (2, 1, 3):
            for copy in own_copies(rb, step, x):
                copy.start()
        c_got[x, rb] = c_part[b, x]
        c_got_lse[x, rb] = c_lse[b, x]

    def start_side(rb):
        for step in (2, 1, 3):
            for copy in side_copies(rb, step, x):
                copy.start()
        b = 4 * (1 - y) + rb
        side[x, rb] = c_part[b, x]
        side_lse[x, rb] = c_lse[b, x]

    def start_joint(rb):
        for step in (1, 2, 3):
            for copy in side_copies(rb, step, peer(step)):
                copy.wait_recv()
        blend(
            [side.at[k, rb] for k in range(ENC)],
            [side_lse.at[k, rb] for k in range(ENC)],
            joint.at[rb],
            joint_lse.at[rb],
        )
        for copy in joint_copies(rb):
            copy.start()

    def add_over(rb):
        b, k = 4 * y + rb, rb - 2
        for copy in over_copies(rb):
            copy.wait_recv()
        for t in range(ENC):
            blend(
                [c_part.at[b, t], over.at[k, t]],
                [c_lse.at[b, t], over_lse.at[k, t]],
                c_part.at[b, t],
                c_lse.at[b, t],
            )

    valid = jnp.where(y == 0, SIZES[1], LAST_VALID)

    def last_loop(j, carry):
        mine = j // 4
        rb = (1 - mine) * (j // 2 + 2 * (j % 2)) + mine * (j % 4)
        chunk = (1 - mine) * (1 - y) + mine * y
        i = 2 * rb + chunk
        b = 4 * chunk + rb
        rows = pl.ds(pl.multiple_of(rb * BLOCK, BLOCK), BLOCK)
        one, two, off = pick[b, 0], pick[b, 1], bias[b]
        bias_one = jnp.where(lax.broadcasted_iota(jnp.int32, (1, SIZES[1]), 1) < valid, 0.0, NEG)
        bias_two = bias_one + off
        before = [top[i, t] for t in range(ENC)]
        k1, k2, v1, v2 = img_b[one, 0], img_b[two, 0], img_b[one, 1], img_b[two, 1]
        queries = [pair(cq.at[t, chunk], rows) for t in range(ENC)]
        scores = [
            (dot_t(q, k1) * EXP_SCALE + bias_one, dot_t(q, k2) * EXP_SCALE + bias_two) for q in queries
        ]
        tops = [jnp.maximum(m, old) for m, old in zip(tops_of(scores), before)]
        mixed = mix(scores, tops, v1, v2)
        fades = [jnp.exp2(old - m) for old, m in zip(before, tops)]
        weighted = [acc[i, t] * fades[t] + mixed[t][:, :HEAD] for t in range(ENC)]
        totals = [tot[i, t] * fades[t] + mixed[t][:, HEAD:] for t in range(ENC)]
        for t in range(ENC):
            put(c_part, c_lse, b, t, weighted[t], totals[t], tops[t])

        for k in (0, 2):

            @pl.when(j == k)
            def _():
                start_side(k // 2)

        for k in (1, 3):

            @pl.when(j == k)
            def _():
                for copy in over_copies(2 + k // 2):
                    copy.start()

        for k in (4, 5):

            @pl.when(j == k)
            def _():
                start_own(k - 4)

        for k in (3, 5):

            @pl.when(j == k)
            def _():
                start_joint(k // 2 - 1)

        @pl.when(j >= 6)
        def _():
            add_over(j - 4)
            start_own(j - 4)

        return carry

    lax.fori_loop(0, 8, last_loop, 0)

    def cross_combine(rb, sources):
        for step in (1, 2, 3):
            for copy in own_copies(rb, step, peer(step)):
                copy.wait_recv()
        if sources > ENC:
            for copy in joint_copies(rb):
                copy.wait_recv()
        combine(c_got, c_got_lse, sources, rb, cross_rows)
        store(cross_rows, 1, rb, 4 + rb).start()

    for rb in (0, 1):
        cross_combine(rb, ENC + 1)
    for rb in (2, 3):
        cross_combine(rb, ENC)

    ring_sent(ring_a)
    ring_sent(ring_b)
    for direction in range(2):
        for distance in range(4):
            if distance < 3 or direction == 0:
                text_unit(direction, distance, distance).wait_send()
    for k in range(LAYERS):
        text_across(k, y).wait_send()
    for which in range(2):
        half_send(which).wait_send()
    seen_copy.wait_send()
    for step in (1, 2, 3):
        sq_copy(step).wait_send()
    for flip in range(2):
        for step in range(ENC):
            if flip or step:
                cq_copy(flip, step).wait_send()

    for rb in range(4):
        for step in (1, 2, 3):
            for copy in s_copies(rb, step):
                copy.wait_send()
            for copy in own_copies(rb, step, x):
                copy.wait_send()
            if rb < 2:
                for copy in side_copies(rb, step, x):
                    copy.wait_send()
        for copy in joint_copies(rb) if rb < 2 else over_copies(rb):
            copy.wait_send()
    for rb in range(4):
        store(self_rows, 0, rb, rb).wait()
        store(cross_rows, 1, rb, 4 + rb).wait()


def per_device(self_query, text_kv, cross_query, image_kv, block_images, image_owner):
    image = jnp.swapaxes(image_kv[0], 0, 1)
    vmem = pl.BlockSpec(memory_space=pltpu.VMEM)
    hbm = pl.BlockSpec(memory_space=pl.ANY)
    smem = pl.BlockSpec(memory_space=pltpu.SMEM)
    dma = pltpu.SemaphoreType.DMA
    both = pl.pallas_call(
        kernel,
        out_shape=jax.ShapeDtypeStruct((2, ROWS, 2 * HEAD), BF),
        in_specs=[hbm, hbm, hbm, hbm, vmem, smem],
        out_specs=hbm,
        scratch_shapes=[
            *(pltpu.VMEM((16, 2, size, HEAD), BF) for size in SIZES),
            pltpu.VMEM((2 * HALF, 2, HEAD), BF),
            pltpu.VMEM((BLOCK, 2, HEAD), BF),
            *(pltpu.VMEM((2, size, HEAD), BF) for size in SIZES),
            pltpu.VMEM((16, BLOCK, 2 * HEAD), BF),
            pltpu.VMEM((ENC, ROWS, 2 * HEAD), BF),
            pltpu.VMEM((ENC, 2, ROWS, 2 * HEAD), BF),
            pltpu.VMEM((2, 8, 128), jnp.int32),
            pltpu.SMEM((2, 8, 128), jnp.int32),
            pltpu.SMEM((8, 2), jnp.int32),
            pltpu.SMEM((8,), F32),
            pltpu.VMEM((8, ENC, TILE, HEAD), F32),
            pltpu.VMEM((8, ENC, TILE, HEAD), F32),
            pltpu.VMEM((8, ENC, TILE, 1), F32),
            pltpu.VMEM((4, ENC, BLOCK, 2 * HEAD), BF),
            pltpu.VMEM((4, ENC, 8, HEAD), F32),
            pltpu.VMEM((ENC, 4, BLOCK, 2 * HEAD), BF),
            pltpu.VMEM((ENC, 4, 8, HEAD), F32),
            pltpu.VMEM((8, ENC, BLOCK, 2 * HEAD), BF),
            pltpu.VMEM((8, ENC, 8, HEAD), F32),
            pltpu.VMEM((ENC + 1, 4, BLOCK, 2 * HEAD), BF),
            pltpu.VMEM((ENC + 1, 4, 8, HEAD), F32),
            pltpu.VMEM((2, ENC, BLOCK, 2 * HEAD), BF),
            pltpu.VMEM((2, ENC, 8, HEAD), F32),
            pltpu.VMEM((ENC, 2, BLOCK, 2 * HEAD), BF),
            pltpu.VMEM((ENC, 2, 8, HEAD), F32),
            pltpu.VMEM((2, BLOCK, 2 * HEAD), BF),
            pltpu.VMEM((2, 8, HEAD), F32),
            dma((2, 4, 2)), dma((2, 4, 2)), dma((2, 4, 2)), dma((2, 4, 2)),
            dma((2, 4)), dma((2, 4)), dma((LAYERS,)), dma((LAYERS,)),
            dma((3,)), dma((3,)),
            dma((ENC,)), dma((ENC,)), dma((2, ENC)), dma((ENC, 2)),
            dma((4, ENC)), dma((ENC, 4)), dma((4, ENC)), dma((ENC, 4)),
            dma((4, ENC)), dma((ENC, 4)), dma((4, ENC)), dma((ENC, 4)),
            dma((2,)), dma((2,)), dma((2,)), dma((2,)),
            dma((2, ENC)), dma((ENC, 2)), dma((2, ENC)), dma((ENC, 2)),
            dma((2,)), dma((2,)), dma((2,)), dma((2,)),
            dma, dma((4,)), dma((8,)),
            pltpu.VMEM((4, BLOCK, 2 * HEAD), BF),
            pltpu.VMEM((4, BLOCK, 2 * HEAD), BF),
        ],
        compiler_params=pltpu.CompilerParams(
            collective_id=0, has_side_effects=True, vmem_limit_bytes=60 * 2**20
        ),
        cost_estimate=pl.CostEstimate(
            flops=512 * 22_000_000, bytes_accessed=8_000_000, transcendentals=22_000_000
        ),
    )(self_query, text_kv, cross_query, image, block_images, image_owner)
    return both[0], both[1]


def solution(mesh):
    spread = P("blk", ("tp", "enc"))
    return jax.shard_map(
        per_device,
        mesh=mesh,
        in_specs=(spread, P("blk", None, "tp"), spread, P("blk", None, "enc", "tp"), P("blk", None), P()),
        out_specs=(spread, spread),
        check_vma=False,
    )
```

```python
import functools
import math

import jax
import jax.numpy as jnp
from jax import lax
from jax.experimental import pallas as pl
from jax.experimental.pallas import tpu as pltpu
from jax.sharding import PartitionSpec as P

MESH = pl.DeviceIdType.MESH
BF = jnp.bfloat16
F32 = jnp.float32
LAYERS = 8
ENC = 4
HEAD = 128
BLOCK = 128
ROWS = 512
TOKENS = 1601
HALF = 816
SIZES = (512, 304)
STARTS = (0, 512)
LAST_VALID = TOKENS - HALF - STARTS[1]
NEG = -1e30
EXP_SCALE = math.log2(math.e) / math.sqrt(HEAD)
TILE = 256


def dot_t(a, b):
    return lax.dot_general(a, b, (((1,), (1,)), ((), ())), preferred_element_type=F32)


def weigh(p, v):
    ones = jnp.ones(v.shape, BF)
    return jnp.dot(p.astype(BF), jnp.concatenate([v, ones], axis=1), preferred_element_type=F32)


def kernel(
    sq_ref, text_ref, cq_ref, img_ref, seen_ref, owner_ref,
    out_ref,
    img_a, img_b, raw, raw_text, stage_a, stage_b, text, sq, cq, seen, seen_sm, pick, bias,
    acc, tot, top,
    s_part, s_lse, s_got, s_got_lse,
    c_part, c_lse, c_got, c_got_lse,
    over, over_lse, side, side_lse, joint, joint_lse,
    za_s, za_r, zb_s, zb_r, tz_s, tz_r, ty_s, ty_r, y_s, y_r,
    sq_s, sq_r, cq_s, cq_r, so_s, so_r, sl_s, sl_r, co_s, co_r, cl_s, cl_r,
    oo_s, oo_r, ol_s, ol_r, do_s, do_r, dl_s, dl_r, jo_s, jo_r, jl_s, jl_r, local_sem, load_sem, store_sem, self_rows, cross_rows,
):
    blk = lax.axis_index("blk")
    x = lax.axis_index("enc")
    z = blk // 2
    y = blk % 2
    partner = 2 * z + 1 - y

    def at(z_, y_, x_):
        return {"blk": 2 * z_ + y_, "enc": x_}

    def remote(src, dst, s, r, device):
        return pltpu.make_async_remote_copy(
            src_ref=src, dst_ref=dst, send_sem=s, recv_sem=r, device_id=device, device_id_type=MESH
        )

    sign = (1, -1)

    def layer(direction, distance):
        return (z - sign[direction] * distance + LAYERS) % LAYERS

    def onward(direction):
        return at((z + sign[direction] + LAYERS) % LAYERS, y, x)

    def unit(buf, s, r, direction, distance, order, sem):
        slot = 2 * layer(direction, distance) + (y + order) % 2
        return remote(
            buf.at[slot], buf.at[slot],
            s.at[direction, sem, order], r.at[direction, sem, order], onward(direction),
        )

    ring_a = (img_a, za_s, za_r)
    ring_b = (img_b, zb_s, zb_r)

    def send_own(ring, order):
        for direction in range(2):
            unit(*ring, direction, 0, order, 0).start()

    def ring_event(ring, distance, order):
        for direction in range(2):
            if distance == 4 and order != direction:
                continue
            unit(*ring, direction, distance, order, distance - 1).wait_recv()
            if distance < 3 or (distance == 3 and order == direction):
                unit(*ring, direction, distance, order, distance).start()

    def ring_last(ring):
        ring_event(ring, 4, 0)
        ring_event(ring, 4, 1)

    def ring_sent(ring):
        for direction in range(2):
            for distance in range(4):
                for order in range(2):
                    if distance < 3 or order == direction:
                        unit(*ring, direction, distance, order, distance).wait_send()

    def text_unit(direction, distance, sem):
        chunk = 2 * layer(direction, distance) + y
        rows = pl.ds(direction * BLOCK // 2, BLOCK // 2) if sem == 3 else pl.ds(0, BLOCK)
        return remote(
            text.at[chunk, rows], text.at[chunk, rows],
            tz_s.at[direction, sem], tz_r.at[direction, sem], onward(direction),
        )

    def text_across(chunk_layer, y_):
        chunk = 2 * chunk_layer + y_
        return remote(
            text.at[chunk], text.at[chunk], ty_s.at[chunk_layer], ty_r.at[chunk_layer],
            {"blk": partner},
        )

    def text_event(distance):
        for direction in range(2):
            text_unit(direction, distance, distance - 1).wait_recv()
            if distance < 4:
                text_unit(direction, distance, distance).start()
                text_across(layer(direction, distance), y).start()
        if distance == 4:
            text_across(layer(0, 4), y).start()

    def peer(step):
        return (x + step) % ENC

    def sq_copy(step):
        return remote(sq_ref, sq.at[x], sq_s.at[step], sq_r.at[x], at(z, y, peer(step)))

    def cq_copy(flip, step):
        return remote(
            cq_ref, cq.at[x, y], cq_s.at[flip, step], cq_r.at[x, y],
            at(z, (y + flip) % 2, peer(step)),
        )

    stages = ((stage_a, img_a), (stage_b, img_b))

    def half_copy(which, slot):
        stage, buf = stages[which]
        return remote(stage, buf.at[slot], y_s.at[which], y_r.at[which], {"blk": partner})

    def half_send(which):
        return half_copy(which, 2 * z + y)

    def half_wait(which):
        half_copy(which, 2 * z + 1 - y).wait_recv()

    seen_copy = remote(seen.at[y], seen.at[y], y_s.at[2], y_r.at[2], {"blk": partner})

    own = 2 * z + y
    quarter = pl.ds(pl.multiple_of(x * BLOCK, BLOCK), BLOCK)
    loads = [
        pltpu.make_async_copy(src, dst, load_sem.at[k])
        for k, (src, dst) in enumerate(
            (
                (img_ref, raw.at[pl.ds(0, TOKENS)]),
                (text_ref.at[quarter], raw_text),
                (sq_ref, sq.at[x]),
                (cq_ref, cq.at[x, y]),
            )
        )
    ]
    for load in loads:
        load.start()
    raw[TOKENS:] = jnp.zeros((2 * HALF - TOKENS, 2, HEAD), BF)

    barrier = pltpu.get_barrier_semaphore()
    for flip in range(2):
        for step in range(ENC):
            if flip or step:
                pl.semaphore_signal(
                    barrier, inc=1, device_id=at(z, (y + flip) % 2, peer(step)), device_id_type=MESH
                )
    for direction in range(2):
        pl.semaphore_signal(barrier, inc=1, device_id=onward(direction), device_id_type=MESH)

    for load in loads:
        load.wait()
    for kv in range(2):
        text[own, :, kv * HEAD : (kv + 1) * HEAD] = raw_text[:, kv, :]
        for which, (stage, buf) in enumerate(stages):
            size = SIZES[which]
            buf[own, kv] = raw[pl.ds(y * HALF + STARTS[which], size), kv, :]
            stage[kv] = raw[pl.ds((1 - y) * HALF + STARTS[which], size), kv, :]
    seen[y] = jnp.zeros((8, 128), jnp.int32)
    seen[y, 0:4, 0:16] = seen_ref[...]

    pl.semaphore_wait(barrier, 9)

    half_send(0).start()
    for direction in range(2):
        text_unit(direction, 0, 0).start()
    send_own(ring_a, 0)
    for step in (1, 3, 2):
        sq_copy(step).start()
    text_event(1)
    half_wait(0)
    send_own(ring_a, 1)
    text_across(z, y).start()
    seen_copy.start()
    half_send(1).start()
    text_event(2)
    ring_event(ring_a, 1, 0)
    cq_copy(1, 0).start()
    text_event(3)
    text_event(4)
    ring_event(ring_a, 1, 1)
    cq_copy(0, 1).start()
    cq_copy(0, 3).start()
    ring_event(ring_a, 2, 0)
    cq_copy(1, 1).start()
    for k in range(LAYERS):
        text_across(k, 1 - y).wait_recv()
    for step in (1, 2, 3):
        other = peer(step)
        remote(sq.at[other], sq.at[other], sq_s.at[step], sq_r.at[other], at(z, y, other)).wait_recv()

    diagonal = lax.broadcasted_iota(jnp.int32, (BLOCK, BLOCK), 0) == lax.broadcasted_iota(
        jnp.int32, (BLOCK, BLOCK), 1
    )

    def pair(ref, rows):
        return jnp.concatenate([ref[rows, 0:HEAD], ref[rows, HEAD : 2 * HEAD]], axis=0)

    def put(part, lse, block, t, weighted, total, level):
        for k in range(2):
            mine = slice(k * BLOCK, (k + 1) * BLOCK)
            part[block, t, :, k * HEAD : (k + 1) * HEAD] = weighted[mine].astype(BF)
            square = jnp.where(diagonal, level[mine], 0.0)
            lse[block, t, k : k + 1, :] = jnp.sum(square, axis=0, keepdims=True)
            square = jnp.where(diagonal, total[mine], 0.0)
            lse[block, t, 2 + k : 3 + k, :] = jnp.sum(square, axis=0, keepdims=True)

    def s_copies(rb, step):
        t = peer(step)
        device = at(z, y, t)
        return (
            remote(s_part.at[rb, t], s_got.at[x, rb], so_s.at[rb, step], so_r.at[x, rb], device),
            remote(s_lse.at[rb, t], s_got_lse.at[x, rb], sl_s.at[rb, step], sl_r.at[x, rb], device),
        )

    def self_step(rb):
        rows = pl.ds(pl.multiple_of(rb * BLOCK, BLOCK), BLOCK)
        keys = text[:, :, 0:HEAD].reshape(16 * BLOCK, HEAD)
        values = text[:, :, HEAD:].reshape(16 * BLOCK, HEAD)
        row = lax.broadcasted_iota(jnp.int32, (TILE, 1), 0) % BLOCK
        inside = jnp.where(x < rb, BLOCK, jnp.where(x == rb, row + 1, 0))
        limit = blk * BLOCK + inside
        index = lax.broadcasted_iota(jnp.int32, (TILE, 16 * BLOCK), 1)
        scores = [jnp.where(index < limit, dot_t(pair(sq.at[t], rows), keys), NEG) for t in range(ENC)]
        tops = [jnp.max(s, axis=1, keepdims=True) * EXP_SCALE for s in scores]
        mixed = [weigh(jnp.exp2(s * EXP_SCALE - m), values) for s, m in zip(scores, tops)]
        for t in range(ENC):
            put(s_part, s_lse, rb, t, mixed[t][:, :HEAD], mixed[t][:, HEAD:], tops[t])
        s_got[x, rb] = s_part[rb, x]
        s_got_lse[x, rb] = s_lse[rb, x]

    def self_loop(i, carry):
        @pl.when(i == 0)
        def _():
            ring_event(ring_a, 2, 1)
            cq_copy(1, 3).start()

        @pl.when(i == 2)
        def _():
            ring_event(ring_a, 3, 0)
            send_own(ring_b, 0)
            cq_copy(0, 2).start()

        @pl.when(i == 3)
        def _():
            ring_event(ring_a, 3, 1)
            half_wait(1)
            send_own(ring_b, 1)
            cq_copy(1, 2).start()

        self_step(i)
        return carry

    lax.fori_loop(0, 4, self_loop, 0)
    ring_last(ring_a)

    remote(seen.at[1 - y], seen.at[1 - y], y_s.at[2], y_r.at[2], {"blk": partner}).wait_recv()
    to_scalar = pltpu.make_async_copy(seen, seen_sm, local_sem)
    to_scalar.start()
    to_scalar.wait()

    def choose(b, carry):
        latest = jnp.int32(0)
        earlier = jnp.int32(0)
        count = jnp.int32(0)
        for i in range(16):
            flag = seen_sm[b // 4, b % 4, i] > 0
            slot = owner_ref[i]
            earlier = jnp.where(jnp.logical_and(flag, count == 0), slot, earlier)
            latest = jnp.where(flag, slot, latest)
            count = count + jnp.where(flag, 1, 0)
        pick[b, 0] = latest
        pick[b, 1] = earlier
        bias[b] = jnp.where(count > 1, 0.0, NEG)
        return carry

    lax.fori_loop(0, 8, choose, 0)
    for flip in range(2):
        for step in range(ENC):
            if flip or step:
                ox, oy = peer(step), (y + flip) % 2
                remote(
                    cq.at[ox, oy], cq.at[ox, oy], cq_s.at[flip, step], cq_r.at[ox, oy], at(z, oy, ox)
                ).wait_recv()

    def block_of(i):
        chunk, rb = i % 2, i // 2
        b = chunk * 4 + rb
        rows = pl.ds(pl.multiple_of(rb * BLOCK, BLOCK), BLOCK)
        return chunk, rb, b, rows, pick[b, 0], pick[b, 1], bias[b]

    def tops_of(scores):
        return [
            jnp.maximum(jnp.max(s1, axis=1, keepdims=True), jnp.max(s2, axis=1, keepdims=True))
            for s1, s2 in scores
        ]

    def mix(scores, tops, v1, v2):
        return [
            weigh(jnp.exp2(s1 - m), v1) + weigh(jnp.exp2(s2 - m), v2)
            for (s1, s2), m in zip(scores, tops)
        ]

    def first_step(i):
        chunk, rb, b, rows, one, two, off = block_of(i)
        k1, k2, v1, v2 = img_a[one, 0], img_a[two, 0], img_a[one, 1], img_a[two, 1]
        queries = [pair(cq.at[t, chunk], rows) for t in range(ENC)]
        scores = [(dot_t(q, k1) * EXP_SCALE, dot_t(q, k2) * EXP_SCALE + off) for q in queries]
        tops = tops_of(scores)
        mixed = mix(scores, tops, v1, v2)
        for t in range(ENC):
            acc[i, t] = mixed[t][:, :HEAD]
            tot[i, t] = mixed[t][:, HEAD:]
            top[i, t] = tops[t]

    def pass_event(k):
        if k < 6:
            ring_event(ring_b, 1 + k // 2, k % 2)
        else:
            ring_last(ring_b)

    def first_loop(i, carry):
        for k in range(7):

            @pl.when(i == k + 1)
            def _():
                pass_event(k)
                if k < 4:
                    for step in (1, 3, 2):
                        for copy in s_copies(k, step):
                            copy.start()

        first_step(i)
        return carry

    lax.fori_loop(0, 8, first_loop, 0)

    def store(rows, which, block, sem):
        place = pl.ds(pl.multiple_of(block * BLOCK, BLOCK), BLOCK)
        return pltpu.make_async_copy(rows.at[block], out_ref.at[which, place, :], store_sem.at[sem])

    def blend(parts, stats, out, stat_out):
        stats = [stat[...] for stat in stats]
        levels = [stat[0:2] for stat in stats]
        high = functools.reduce(jnp.maximum, levels)
        shares = [jnp.exp2(level - high) for level in levels]
        total = functools.reduce(jnp.add, [s * stat[2:4] for s, stat in zip(shares, stats)])
        if stat_out is None:
            shares = [share / total for share in shares]
        else:
            stat_out[0:2, :] = high
            stat_out[2:4, :] = total
        for hh in range(2):
            lanes = slice(hh * HEAD, (hh + 1) * HEAD)
            mixed = jnp.zeros((BLOCK, HEAD), F32)
            for part, share in zip(parts, shares):
                line = jnp.broadcast_to(share[hh : hh + 1], (BLOCK, BLOCK))
                column = jnp.sum(jnp.where(diagonal, line, 0.0), axis=1, keepdims=True)
                mixed = mixed + part[:, lanes].astype(F32) * column
            out[:, lanes] = mixed.astype(BF)

    def combine(got, got_lse, sources, block, rows):
        blend(
            [got.at[k, block] for k in range(sources)],
            [got_lse.at[k, block] for k in range(sources)],
            rows.at[block],
            None,
        )

    def self_combine(rb, carry):
        for step in (1, 2, 3):
            o = peer(step)
            device = at(z, y, o)
            remote(s_part.at[rb, o], s_got.at[o, rb], so_s.at[rb, step], so_r.at[o, rb], device).wait_recv()
            remote(s_lse.at[rb, o], s_got_lse.at[o, rb], sl_s.at[rb, step], sl_r.at[o, rb], device).wait_recv()
        combine(s_got, s_got_lse, 4, rb, self_rows)
        store(self_rows, 0, rb, rb).start()
        return carry

    lax.fori_loop(0, 4, self_combine, 0)

    def pairs(src, src_lse, dst, dst_lse, so, ro, sl, rl, device):
        return (remote(src, dst, so, ro, device), remote(src_lse, dst_lse, sl, rl, device))

    def own_copies(rb, step, source):
        t, b = peer(step), 4 * y + rb
        return pairs(
            c_part.at[b, t], c_lse.at[b, t], c_got.at[source, rb], c_got_lse.at[source, rb],
            co_s.at[rb, step], co_r.at[source, rb], cl_s.at[rb, step], cl_r.at[source, rb], at(z, y, t),
        )

    def side_copies(rb, step, source):
        t, b = peer(step), 4 * (1 - y) + rb
        return pairs(
            c_part.at[b, t], c_lse.at[b, t], side.at[source, rb], side_lse.at[source, rb],
            do_s.at[rb, step], do_r.at[source, rb], dl_s.at[rb, step], dl_r.at[source, rb], at(z, y, t),
        )

    def over_copies(rb):
        b, k = 4 * (1 - y) + rb, rb - 2
        return pairs(
            c_part.at[b], c_lse.at[b], over.at[k], over_lse.at[k],
            oo_s.at[k], oo_r.at[k], ol_s.at[k], ol_r.at[k], {"blk": partner},
        )

    def joint_copies(rb):
        return pairs(
            joint.at[rb], joint_lse.at[rb], c_got.at[ENC, rb], c_got_lse.at[ENC, rb],
            jo_s.at[rb], jo_r.at[rb], jl_s.at[rb], jl_r.at[rb], {"blk": partner},
        )

    def start_own(rb):
        b = 4 * y + rb
        for step in (2, 1, 3):
            for copy in own_copies(rb, step, x):
                copy.start()
        c_got[x, rb] = c_part[b, x]
        c_got_lse[x, rb] = c_lse[b, x]

    def start_side(rb):
        for step in (2, 1, 3):
            for copy in side_copies(rb, step, x):
                copy.start()
        b = 4 * (1 - y) + rb
        side[x, rb] = c_part[b, x]
        side_lse[x, rb] = c_lse[b, x]

    def start_joint(rb):
        for step in (1, 2, 3):
            for copy in side_copies(rb, step, peer(step)):
                copy.wait_recv()
        blend(
            [side.at[k, rb] for k in range(ENC)],
            [side_lse.at[k, rb] for k in range(ENC)],
            joint.at[rb],
            joint_lse.at[rb],
        )
        for copy in joint_copies(rb):
            copy.start()

    def add_over(rb):
        b, k = 4 * y + rb, rb - 2
        for copy in over_copies(rb):
            copy.wait_recv()
        for t in range(ENC):
            blend(
                [c_part.at[b, t], over.at[k, t]],
                [c_lse.at[b, t], over_lse.at[k, t]],
                c_part.at[b, t],
                c_lse.at[b, t],
            )

    valid = jnp.where(y == 0, SIZES[1], LAST_VALID)

    def last_loop(j, carry):
        mine = j // 4
        rb = (1 - mine) * (j // 2 + 2 * (j % 2)) + mine * (j % 4)
        chunk = (1 - mine) * (1 - y) + mine * y
        i = 2 * rb + chunk
        b = 4 * chunk + rb
        rows = pl.ds(pl.multiple_of(rb * BLOCK, BLOCK), BLOCK)
        one, two, off = pick[b, 0], pick[b, 1], bias[b]
        bias_one = jnp.where(lax.broadcasted_iota(jnp.int32, (1, SIZES[1]), 1) < valid, 0.0, NEG)
        bias_two = bias_one + off
        before = [top[i, t] for t in range(ENC)]
        k1, k2, v1, v2 = img_b[one, 0], img_b[two, 0], img_b[one, 1], img_b[two, 1]
        queries = [pair(cq.at[t, chunk], rows) for t in range(ENC)]
        scores = [
            (dot_t(q, k1) * EXP_SCALE + bias_one, dot_t(q, k2) * EXP_SCALE + bias_two) for q in queries
        ]
        tops = [jnp.maximum(m, old) for m, old in zip(tops_of(scores), before)]
        mixed = mix(scores, tops, v1, v2)
        fades = [jnp.exp2(old - m) for old, m in zip(before, tops)]
        weighted = [acc[i, t] * fades[t] + mixed[t][:, :HEAD] for t in range(ENC)]
        totals = [tot[i, t] * fades[t] + mixed[t][:, HEAD:] for t in range(ENC)]
        for t in range(ENC):
            put(c_part, c_lse, b, t, weighted[t], totals[t], tops[t])

        for k in (0, 2):

            @pl.when(j == k)
            def _():
                start_side(k // 2)

        for k in (1, 3):

            @pl.when(j == k)
            def _():
                for copy in over_copies(2 + k // 2):
                    copy.start()

        for k in (4, 5):

            @pl.when(j == k)
            def _():
                start_own(k - 4)

        for k in (3, 5):

            @pl.when(j == k)
            def _():
                start_joint(k // 2 - 1)

        @pl.when(j >= 6)
        def _():
            add_over(j - 4)
            start_own(j - 4)

        return carry

    lax.fori_loop(0, 8, last_loop, 0)

    def cross_combine(rb, sources):
        for step in (1, 2, 3):
            for copy in own_copies(rb, step, peer(step)):
                copy.wait_recv()
        if sources > ENC:
            for copy in joint_copies(rb):
                copy.wait_recv()
        combine(c_got, c_got_lse, sources, rb, cross_rows)
        store(cross_rows, 1, rb, 4 + rb).start()

    for rb in (0, 1):
        cross_combine(rb, ENC + 1)
    for rb in (2, 3):
        cross_combine(rb, ENC)

    ring_sent(ring_a)
    ring_sent(ring_b)
    for direction in range(2):
        for distance in range(4):
            text_unit(direction, distance, distance).wait_send()
    for k in range(LAYERS):
        text_across(k, y).wait_send()
    for which in range(2):
        half_send(which).wait_send()
    seen_copy.wait_send()
    for step in (1, 2, 3):
        sq_copy(step).wait_send()
    for flip in range(2):
        for step in range(ENC):
            if flip or step:
                cq_copy(flip, step).wait_send()

    for rb in range(4):
        for step in (1, 2, 3):
            for copy in s_copies(rb, step):
                copy.wait_send()
            for copy in own_copies(rb, step, x):
                copy.wait_send()
            if rb < 2:
                for copy in side_copies(rb, step, x):
                    copy.wait_send()
        for copy in joint_copies(rb) if rb < 2 else over_copies(rb):
            copy.wait_send()
    for rb in range(4):
        store(self_rows, 0, rb, rb).wait()
        store(cross_rows, 1, rb, 4 + rb).wait()


def per_device(self_query, text_kv, cross_query, image_kv, block_images, image_owner):
    image = jnp.swapaxes(image_kv[0], 0, 1)
    vmem = pl.BlockSpec(memory_space=pltpu.VMEM)
    hbm = pl.BlockSpec(memory_space=pl.ANY)
    smem = pl.BlockSpec(memory_space=pltpu.SMEM)
    dma = pltpu.SemaphoreType.DMA
    both = pl.pallas_call(
        kernel,
        out_shape=jax.ShapeDtypeStruct((2, ROWS, 2 * HEAD), BF),
        in_specs=[hbm, hbm, hbm, hbm, vmem, smem],
        out_specs=hbm,
        scratch_shapes=[
            *(pltpu.VMEM((16, 2, size, HEAD), BF) for size in SIZES),
            pltpu.VMEM((2 * HALF, 2, HEAD), BF),
            pltpu.VMEM((BLOCK, 2, HEAD), BF),
            *(pltpu.VMEM((2, size, HEAD), BF) for size in SIZES),
            pltpu.VMEM((16, BLOCK, 2 * HEAD), BF),
            pltpu.VMEM((ENC, ROWS, 2 * HEAD), BF),
            pltpu.VMEM((ENC, 2, ROWS, 2 * HEAD), BF),
            pltpu.VMEM((2, 8, 128), jnp.int32),
            pltpu.SMEM((2, 8, 128), jnp.int32),
            pltpu.SMEM((8, 2), jnp.int32),
            pltpu.SMEM((8,), F32),
            pltpu.VMEM((8, ENC, TILE, HEAD), F32),
            pltpu.VMEM((8, ENC, TILE, HEAD), F32),
            pltpu.VMEM((8, ENC, TILE, 1), F32),
            pltpu.VMEM((4, ENC, BLOCK, 2 * HEAD), BF),
            pltpu.VMEM((4, ENC, 8, HEAD), F32),
            pltpu.VMEM((ENC, 4, BLOCK, 2 * HEAD), BF),
            pltpu.VMEM((ENC, 4, 8, HEAD), F32),
            pltpu.VMEM((8, ENC, BLOCK, 2 * HEAD), BF),
            pltpu.VMEM((8, ENC, 8, HEAD), F32),
            pltpu.VMEM((ENC + 1, 4, BLOCK, 2 * HEAD), BF),
            pltpu.VMEM((ENC + 1, 4, 8, HEAD), F32),
            pltpu.VMEM((2, ENC, BLOCK, 2 * HEAD), BF),
            pltpu.VMEM((2, ENC, 8, HEAD), F32),
            pltpu.VMEM((ENC, 2, BLOCK, 2 * HEAD), BF),
            pltpu.VMEM((ENC, 2, 8, HEAD), F32),
            pltpu.VMEM((2, BLOCK, 2 * HEAD), BF),
            pltpu.VMEM((2, 8, HEAD), F32),
            dma((2, 4, 2)), dma((2, 4, 2)), dma((2, 4, 2)), dma((2, 4, 2)),
            dma((2, 4)), dma((2, 4)), dma((LAYERS,)), dma((LAYERS,)),
            dma((3,)), dma((3,)),
            dma((ENC,)), dma((ENC,)), dma((2, ENC)), dma((ENC, 2)),
            dma((4, ENC)), dma((ENC, 4)), dma((4, ENC)), dma((ENC, 4)),
            dma((4, ENC)), dma((ENC, 4)), dma((4, ENC)), dma((ENC, 4)),
            dma((2,)), dma((2,)), dma((2,)), dma((2,)),
            dma((2, ENC)), dma((ENC, 2)), dma((2, ENC)), dma((ENC, 2)),
            dma((2,)), dma((2,)), dma((2,)), dma((2,)),
            dma, dma((4,)), dma((8,)),
            pltpu.VMEM((4, BLOCK, 2 * HEAD), BF),
            pltpu.VMEM((4, BLOCK, 2 * HEAD), BF),
        ],
        compiler_params=pltpu.CompilerParams(
            collective_id=0, has_side_effects=True, vmem_limit_bytes=60 * 2**20
        ),
        cost_estimate=pl.CostEstimate(
            flops=512 * 22_000_000, bytes_accessed=8_000_000, transcendentals=22_000_000
        ),
    )(self_query, text_kv, cross_query, image, block_images, image_owner)
    return both[0], both[1]


def solution(mesh):
    spread = P("blk", ("tp", "enc"))
    return jax.shard_map(
        per_device,
        mesh=mesh,
        in_specs=(spread, P("blk", None, "tp"), spread, P("blk", None, "enc", "tp"), P("blk", None), P()),
        out_specs=(spread, spread),
        check_vma=False,
    )
```
